32 devices in a mesh: fsdp: 4 (over z), ctx: 4 (over y, x), tp: 2 (over core).
Axes of the slice: x: 2, y: 2, z: 4, core: 2. Of those that a mesh axis runs over, the one named last changes fastest.
Arguments:
- tokens: bfloat16 [4, 4096, 1024], P('fsdp', 'ctx'), may hold values from -6 to 6
- doc_ids: int32 [4, 4096], P('fsdp', 'ctx'), may hold values from 0 to 2, as said below
- prenorm: bfloat16 [1024], P('fsdp'), may hold values from 0.5 to 1.5
- w_query: bfloat16 [1024, 512], P('fsdp', 'tp'), may hold values from -0.1875 to 0.1875
- w_key: bfloat16 [1024, 512], P('fsdp', 'tp'), may hold values from -0.1875 to 0.1875
- w_value: bfloat16 [1024, 1024], P('fsdp', 'tp'), may hold values from -0.1875 to 0.1875
- w_outgate: bfloat16 [1024, 1024], P('fsdp', 'tp'), may hold values from -0.1875 to 0.1875
- w_lowrank: bfloat16 [1024, 16], P('fsdp'), may hold values from -0.1875 to 0.1875
- w_decay: bfloat16 [16, 512], P(None, 'tp'), may hold values from -1.5 to 1.5
- decay_bias: bfloat16 [512], P('tp'), may hold values from -2 to 5
- headnorm: bfloat16 [256], replicated, may hold values from 0.5 to 1.5
- w_output: bfloat16 [1024, 1024], P('tp', 'fsdp'), may hold values from -0.375 to 0.375
- postnorm: bfloat16 [1024], P('fsdp'), may hold values from 0.5 to 1.5
- w_gate: bfloat16 [1024, 2816], P('fsdp', 'tp'), may hold values from -0.1875 to 0.1875
- w_up: bfloat16 [1024, 2816], P('fsdp', 'tp'), may hold values from -0.1875 to 0.1875
- w_down: bfloat16 [2816, 1024], P('tp', 'fsdp'), may hold values from -0.21875 to 0.21875
- cotangent: bfloat16 [4, 4096, 1024], P('fsdp', 'ctx'), may hold values from -6 to 6
Outputs:
- block_out: bfloat16 [4, 4096, 1024], P('fsdp', 'ctx')
- grad_tokens: bfloat16 [4, 4096, 1024], P('fsdp', 'ctx')
- grad_prenorm: float32 [1024], P('fsdp')
- grad_query: float32 [1024, 512], P('fsdp', 'tp')
- grad_key: float32 [1024, 512], P('fsdp', 'tp')
- grad_value: float32 [1024, 1024], P('fsdp', 'tp')
- grad_outgate: float32 [1024, 1024], P('fsdp', 'tp')
- grad_lowrank: float32 [1024, 16], P('fsdp')
- grad_decay: float32 [16, 512], P(None, 'tp')
- grad_bias: float32 [512], P('tp')
- grad_headnorm: float32 [256], replicated
- grad_output: float32 [1024, 1024], P('tp', 'fsdp')
- grad_postnorm: float32 [1024], P('fsdp')
- grad_gate: float32 [1024, 2816], P('fsdp', 'tp')
- grad_up: float32 [1024, 2816], P('fsdp', 'tp')
- grad_down: float32 [2816, 1024], P('tp', 'fsdp')
The draws below stay inside these ranges and needn't reach their ends.
Inputs may be any that keep to these rules, and one draw needn't show every extreme that they name: `doc_ids`: every sequence holds three documents numbered 0, 1, 2 in order. Document 0 begins the sequence and ends within its first 1024 tokens; document 2 begins within its last 1024 tokens and ends it; documents 0 and 2 have 200 tokens or more.
All inputs are finite; a program needn't handle non-finite values.
Results may differ from the reference program's by a relative error of at most 0.029.
Values may be sent and summed in bfloat16 or wider, within the bound.
A program may use at most 128 MiB of HBM per device.

```python
import jax
import jax.numpy as jnp
from jax import lax

D = 1024
HEADS = 4
KD = 512
VD = 1024
LR = 16
FF = 2816
KH = 128
VH = 256
BLOCK = 64
LEN = 4096
MIN_DOC = 200
SEQ_DEV = 1
SEQS = 4
N_CTX = 4


def draw_doc_ids(key, part):
    key = jax.random.fold_in(key, 11)
    first_key, second_key = jax.random.split(key, 2)
    piece_len = LEN // N_CTX
    first_cut = jax.random.randint(first_key, (SEQS,), MIN_DOC, piece_len)
    second_cut = jax.random.randint(second_key, (SEQS,), LEN - piece_len + 1, LEN - MIN_DOC + 1)
    positions = jnp.arange(LEN, dtype=jnp.int32)
    numbers = (positions[None, :] >= first_cut[:, None]).astype(jnp.int32) + (positions[None, :] >= second_cut[:, None]).astype(jnp.int32)
    return numbers.astype(jnp.int32)


def steps_of(rng, shape, cuts, smallest, largest):
    def one(axis_at, blocks):
        steps = jax.random.uniform(jax.random.fold_in(jax.random.fold_in(rng, 6), axis_at), (blocks,), jnp.float32, smallest / len(cuts), largest / len(cuts))
        return jnp.repeat(jnp.exp(steps), shape[axis_at] // blocks).reshape((-1,) + (1,) * (len(shape) - axis_at - 1))

    loudness = one(*cuts[0])
    for cut in cuts[1:]:
        loudness = loudness * one(*cut)
    return loudness


def normal_values(own_key, dims, spread, limit, cuts=(), held_as=jnp.bfloat16):
    entries = spread * jax.random.normal(own_key, dims, jnp.float32)
    if cuts:
        entries = entries * steps_of(own_key, dims, cuts, -0.22, 0.18)
    return jnp.clip(entries, -limit, limit).astype(held_as)


def setup_inputs(seed: int = 0) -> dict:
    keys = jax.random.split(jax.random.key(seed), 18)
    tokens = normal_values(keys[0], (SEQS, LEN, D), 1.0, 6.0, ((0, 4), (1, 4)))
    doc_ids = draw_doc_ids(jax.random.fold_in(keys[17], 71), 0)
    prenorm = jnp.clip(1.0 + 0.1 * jax.random.normal(keys[2], (D,), jnp.float32), 0.5, 1.5).astype(jnp.bfloat16)
    w_query = normal_values(keys[3], (D, KD), D ** -0.5, 0.1875, ((0, 4), (1, 2)))
    w_key = normal_values(keys[4], (D, KD), D ** -0.5, 0.1875, ((0, 4), (1, 2)))
    w_value = normal_values(keys[5], (D, VD), D ** -0.5, 0.1875, ((0, 4), (1, 2)))
    w_outgate = normal_values(keys[6], (D, VD), D ** -0.5, 0.1875, ((0, 4), (1, 2)))
    w_lowrank = normal_values(keys[7], (D, LR), D ** -0.5, 0.1875, ((0, 4),))
    w_decay = normal_values(keys[8], (LR, KD), LR ** -0.5, 1.5, ((1, 2),))
    decay_bias = jnp.clip(-2.0 + 7.0 * jax.random.uniform(keys[9], (KD,), jnp.float32) ** steps_of(keys[9], (KD,), ((0, 2),), -0.2, 0.2), -2.0, 5.0).astype(jnp.bfloat16)
    headnorm = jnp.clip(1.0 + 0.1 * jax.random.normal(keys[10], (VH,), jnp.float32), 0.5, 1.5).astype(jnp.bfloat16)
    w_output = normal_values(keys[11], (VD, D), (VD // 4) ** -0.5, 0.375, ((0, 2), (1, 4)))
    postnorm = jnp.clip(1.0 + 0.1 * jax.random.normal(keys[12], (D,), jnp.float32), 0.5, 1.5).astype(jnp.bfloat16)
    w_gate = normal_values(keys[13], (D, FF), D ** -0.5, 0.1875, ((0, 4), (1, 2)))
    w_up = normal_values(keys[14], (D, FF), D ** -0.5, 0.1875, ((0, 4), (1, 2)))
    w_down = normal_values(keys[15], (FF, D), (FF // 4) ** -0.5, 0.21875, ((0, 2), (1, 4)))
    cotangent = normal_values(keys[16], (SEQS, LEN, D), 1.0, 6.0, ((0, 4), (1, 4)))
    return dict(tokens=tokens, doc_ids=doc_ids, prenorm=prenorm, w_query=w_query, w_key=w_key, w_value=w_value, w_outgate=w_outgate, w_lowrank=w_lowrank, w_decay=w_decay, decay_bias=decay_bias, headnorm=headnorm, w_output=w_output, postnorm=postnorm, w_gate=w_gate, w_up=w_up, w_down=w_down, cotangent=cotangent)


EPSILON = 1e-06
HEAD_FLOOR = 1.0
NORMALIZER = 16.0

@jax.custom_vjp
def low(v):
    return lax.optimization_barrier(v.astype(jnp.bfloat16)).astype(jnp.float32)

@jax.custom_vjp
def low_back(v):
    return v

def low_keep(v):
    return (low(v), None)

def low_pass(kept, grad):
    return (grad,)

def back_keep(v):
    return (v, None)

def back_low(kept, grad):
    return (low(grad),)
low.defvjp(low_keep, low_pass)
low_back.defvjp(back_keep, back_low)

def matmul_high(left, right):
    return jnp.matmul(left, right, precision=lax.Precision.HIGHEST)

def block_step(carry, blocks):
    running, prev_ids = carry
    query_rows, key_rows, value_rows, decay_rows, id_rows = blocks
    total = jnp.cumsum(decay_rows, axis=2)
    block_len = id_rows.shape[1]
    later = lax.broadcasted_iota(jnp.int32, (block_len, block_len), 0)
    earlier = lax.broadcasted_iota(jnp.int32, (block_len, block_len), 1)
    linked = (id_rows[:, :, None] == id_rows[:, None, :]) & (later >= earlier)[None, :, :]
    anchor = total[:, :, block_len // 2:block_len // 2 + 1, :]
    query_scaled = query_rows * jnp.exp(total - anchor)
    key_scaled = key_rows * jnp.exp(anchor - total)
    raw = jnp.einsum('bhtk,bhsk->bhts', query_scaled, key_scaled, precision=lax.Precision.HIGHEST)
    scores = jnp.where(linked[:, None, :, :], raw, 0.0)
    inner = jnp.einsum('bhts,bhsv->bhtv', scores, value_rows, precision=lax.Precision.HIGHEST)
    alive = (id_rows == prev_ids[:, None]).astype(total.dtype)
    reach = query_rows * jnp.exp(total) * alive[:, None, :, None]
    carried = jnp.einsum('bhtk,bhkv->bhtv', reach, running, precision=lax.Precision.HIGHEST)
    last_ids = id_rows[:, -1]
    keep = (id_rows == last_ids[:, None]).astype(total.dtype)
    tail = jnp.exp(total[:, :, -1:, :] - total) * keep[:, None, :, None]
    fresh = jnp.einsum('bhsk,bhsv->bhkv', key_rows * tail, value_rows, precision=lax.Precision.HIGHEST)
    survive = (last_ids == prev_ids).astype(total.dtype)
    running = survive[:, None, None, None] * jnp.exp(total[:, :, -1, :])[:, :, :, None] * running + fresh
    return ((running, last_ids), inner + carried)

def run_blocks(query_all, key_all, value_all, decay_all, doc_rows, running, prev_ids):
    seq_count, head_count, length_all, key_size = query_all.shape
    value_size = value_all.shape[-1]
    count_blocks = length_all // BLOCK

    def split_rows(array):
        return jnp.moveaxis(array.reshape(seq_count, head_count, count_blocks, BLOCK, array.shape[-1]), 2, 0)
    id_blocks = jnp.moveaxis(doc_rows.reshape(seq_count, count_blocks, BLOCK), 1, 0)
    _, outputs = lax.scan(jax.checkpoint(block_step), (running, prev_ids), (split_rows(query_all), split_rows(key_all), split_rows(value_all), split_rows(decay_all), id_blocks))
    return jnp.moveaxis(outputs, 0, 2).reshape(seq_count, head_count, length_all, value_size)

def to_heads(array, size):
    return jnp.transpose(array.reshape(array.shape[0], array.shape[1], -1, size), (0, 2, 1, 3))

def rms_scale(rows):
    return lax.rsqrt(lax.optimization_barrier(jnp.mean(rows * rows, axis=-1, keepdims=True)) + EPSILON)

def head_scale_of(rows):
    return lax.rsqrt(lax.optimization_barrier(jnp.mean(rows * rows, axis=-1, keepdims=True)) + HEAD_FLOOR)

def forward(resid_in, doc_rows, gain_one, mat_query, mat_key, mat_value, mat_outgate, mat_lowrank, mat_decay, bias_decay, gain_head, mat_output, gain_two, mat_gate, mat_up, mat_down):
    seq_count, length_all, model_width = resid_in.shape
    normed_one = low(resid_in * rms_scale(resid_in) * gain_one)
    queries = low(low_back(matmul_high(normed_one, mat_query)))
    key_lin = low(low_back(matmul_high(normed_one, mat_key)))
    values = low(low_back(matmul_high(normed_one, mat_value)))
    gate_pre = low_back(matmul_high(normed_one, mat_outgate))
    rank_act = low(low_back(matmul_high(normed_one, mat_lowrank)))
    decay_logit = low_back(matmul_high(rank_act, mat_decay) + bias_decay)
    log_decay = jax.nn.log_sigmoid(decay_logit) / NORMALIZER
    running = jnp.zeros((seq_count, HEADS, KH, VH), jnp.float32)
    prev_ids = jnp.full((seq_count,), -1, jnp.int32)
    mixed = run_blocks(to_heads(queries, KH) * KH ** (-0.5), to_heads(key_lin, KH), to_heads(values, VH), to_heads(log_decay, KH), doc_rows, running, prev_ids)
    mix_rows = jnp.transpose(mixed, (0, 2, 1, 3))
    unit_rows = mix_rows * head_scale_of(mix_rows)
    gate_rows = gate_pre.reshape(mix_rows.shape)
    gated = low(unit_rows * gain_head * gate_rows * jax.nn.sigmoid(gate_rows))
    attn_out = low_back(matmul_high(gated.reshape(seq_count, length_all, VD), mat_output))
    resid_mid = resid_in + attn_out
    normed_two = low(resid_mid * rms_scale(resid_mid) * gain_two)
    gate_act = low_back(matmul_high(normed_two, mat_gate))
    up_act = low_back(matmul_high(normed_two, mat_up))
    hidden = low(jax.nn.silu(gate_act) * up_act)
    ffn_out = low_back(matmul_high(hidden, mat_down))
    return resid_mid + ffn_out

def reference(tokens, doc_ids, prenorm, w_query, w_key, w_value, w_outgate, w_lowrank, w_decay, decay_bias, headnorm, w_output, postnorm, w_gate, w_up, w_down, cotangent):
    params = tuple((array.astype(jnp.float32) for array in (prenorm, w_query, w_key, w_value, w_outgate, w_lowrank, w_decay, decay_bias, headnorm, w_output, postnorm, w_gate, w_up, w_down)))
    groups = tokens.shape[0] // SEQ_DEV
    token_groups = tokens.reshape(groups, SEQ_DEV, LEN, D)
    id_groups = doc_ids.reshape(groups, SEQ_DEV, LEN)
    cot_groups = cotangent.reshape(groups, SEQ_DEV, LEN, D)

    def group_step(totals, inputs):
        token_part, id_part, cot_part = inputs

        def closed(resid_in, *weights):
            return forward(resid_in, id_part, *weights)
        result, pullback = jax.vjp(closed, token_part.astype(jnp.float32), *params)
        grads = pullback(cot_part.astype(jnp.float32))
        totals = tuple((total + grad for total, grad in zip(totals, grads[1:])))
        return (totals, (result.astype(jnp.bfloat16), grads[0].astype(jnp.bfloat16)))
    start = tuple((jnp.zeros_like(param) for param in params))
    totals, (results, token_grads) = lax.scan(group_step, start, (token_groups, id_groups, cot_groups))
    return (results.reshape(tokens.shape), token_grads.reshape(tokens.shape), totals[0], totals[1], totals[2], totals[3], totals[4], totals[5], totals[6], totals[7], totals[8], totals[9], totals[10], totals[11], totals[12], totals[13])
```

```python
import functools

import jax
import jax.numpy as jnp
from jax import lax
from jax.experimental import pallas as pl
from jax.experimental.pallas import tpu as pltpu
from jax.sharding import PartitionSpec as P

KH = 128
VH = 256
BLOCK = 64


EPSILON = 1e-06
HEAD_FLOOR = 1.0
NORMALIZER = 16.0
SCALE = KH ** (-0.5)
BF = jnp.bfloat16
F32 = jnp.float32
VMEM_LIMIT = 50 * 1024 * 1024


def mm(left, right, left_dim=1, right_dim=0):
    return lax.dot_general(
        left, right, (((left_dim,), (right_dim,)), ((), ())), preferred_element_type=F32
    )


def split_hi_lo(array):
    hi = array.astype(BF)
    return hi, (array - hi.astype(F32)).astype(BF)


def tri(rows, inclusive_lower, copies):
    at_row = lax.broadcasted_iota(jnp.int32, (rows, rows), 0)
    at_col = lax.broadcasted_iota(jnp.int32, (rows, rows), 1)
    mask = at_row >= at_col if inclusive_lower else at_row <= at_col
    square = mask.astype(F32).astype(BF)
    return jnp.concatenate([square] * copies, axis=1)


def block_ids(ids_smem, prev_smem, block):
    last = ids_smem[block * BLOCK + BLOCK - 1]
    before = ids_smem[jnp.maximum(block * BLOCK - 1, 0)]
    prev = jnp.where(block == 0, prev_smem[0], before)
    return last, prev


def ending_kernel(heads, ids_s, prev_s, ids_c, key, value, decay, total_out, state_out, sum_out):
    count = key.shape[0] // BLOCK
    state_out[...] = jnp.zeros_like(state_out)
    sum_out[...] = jnp.zeros_like(sum_out)
    lower = tri(BLOCK, True, 3)

    def step(block, _):
        rows = pl.ds(pl.multiple_of(block * BLOCK, BLOCK), BLOCK)
        last, prev = block_ids(ids_s, prev_s, block)
        keep = (ids_c[rows, :] == last).astype(F32)
        survive = (last == prev).astype(F32)
        decay_rows = decay[rows, :]
        hi, rest = decay_rows.astype(BF), decay_rows
        rest = rest - hi.astype(F32)
        mid, low = split_hi_lo(rest)
        total = mm(lower, jnp.concatenate([hi, mid, low], axis=0))
        total_out[rows, :] = total
        final = total[BLOCK - 1 : BLOCK, :]
        sum_out[...] += final
        tail = (key[rows, :].astype(F32) * jnp.exp(final - total) * keep).astype(BF)
        through = survive * jnp.exp(final)
        for head in range(heads):
            kc = slice(head * KH, (head + 1) * KH)
            vc = slice(head * VH, (head + 1) * VH)
            fresh = mm(value[rows, vc], tail[:, kc], 0, 0)
            state_out[vc, :] = state_out[vc, :] * through[:, kc] + fresh
        return 0

    lax.fori_loop(0, count, step, 0, unroll=4)


def forward_kernel(
    heads,
    ids_s,
    prev_s,
    ids_c,
    ids_r,
    query,
    key,
    value,
    total_in,
    gate,
    gain,
    state_in,
    mixed_out,
    gated_out,
    states_out,
    state,
):
    count = key.shape[0] // BLOCK
    state[...] = state_in[...]
    later = lax.broadcasted_iota(jnp.int32, (BLOCK, BLOCK), 0)
    earlier = lax.broadcasted_iota(jnp.int32, (BLOCK, BLOCK), 1)

    def step(block, _):
        rows = pl.ds(pl.multiple_of(block * BLOCK, BLOCK), BLOCK)
        last, prev = block_ids(ids_s, prev_s, block)
        ids = ids_c[rows, :]
        linked = (ids == ids_r[pl.ds(block, 1), :]) & (later >= earlier)
        keep = (ids == last).astype(F32)
        alive = (ids == prev).astype(F32) * SCALE
        survive = (last == prev).astype(F32)
        total = total_in[rows, :]
        final = total[BLOCK - 1 : BLOCK, :]
        anchor = total[BLOCK // 2 : BLOCK // 2 + 1, :]
        query_f = query[rows, :].astype(F32)
        key_f = key[rows, :].astype(F32)
        query_scaled = (query_f * SCALE * jnp.exp(total - anchor)).astype(BF)
        key_scaled = (key_f * jnp.exp(anchor - total)).astype(BF)
        reach = (query_f * jnp.exp(total) * alive).astype(BF)
        tail = (key_f * jnp.exp(final - total) * keep).astype(BF)
        through = survive * jnp.exp(final)
        for head in range(heads):
            kc = slice(head * KH, (head + 1) * KH)
            vc = slice(head * VH, (head + 1) * VH)
            value_rows = value[rows, vc]
            scores = mm(query_scaled[:, kc], key_scaled[:, kc], 1, 1)
            scores = jnp.where(linked, scores, 0.0).astype(BF)
            now = state[vc, :]
            now_b = now.astype(BF)
            states_out[block, vc, :] = now_b
            out = mm(scores, value_rows) + mm(reach[:, kc], now_b, 1, 1)
            mixed_out[rows, vc] = out
            state[vc, :] = now * through[:, kc] + mm(value_rows, tail[:, kc], 0, 0)
            unit = out * lax.rsqrt(jnp.mean(out * out, axis=-1, keepdims=True) + HEAD_FLOOR)
            gate_rows = gate[rows, vc]
            swish = gate_rows * jax.nn.sigmoid(gate_rows)
            gated_out[rows, vc] = (unit * gain[...] * swish).astype(BF)
        return 0

    lax.fori_loop(0, count, step, 0, unroll=4)


def back_start_kernel(
    heads,
    ids_s,
    prev_s,
    ids_c,
    query,
    total_in,
    gate,
    gain,
    mixed,
    grad_gated,
    grad_mixed_out,
    grad_gate_out,
    headnorm_out,
    adjoint_out,
):
    count = query.shape[0] // BLOCK
    adjoint_out[...] = jnp.zeros_like(adjoint_out)
    headnorm_out[...] = jnp.zeros_like(headnorm_out)

    def step(turn, _):
        block = count - 1 - turn
        rows = pl.ds(pl.multiple_of(block * BLOCK, BLOCK), BLOCK)
        last, prev = block_ids(ids_s, prev_s, block)
        alive = (ids_c[rows, :] == prev).astype(F32) * SCALE
        survive = (last == prev).astype(F32)
        total = total_in[rows, :]
        final = total[BLOCK - 1 : BLOCK, :]
        reach = (query[rows, :].astype(F32) * jnp.exp(total) * alive).astype(BF)
        through = survive * jnp.exp(final)
        gain_row = gain[...]
        for head in range(heads):
            kc = slice(head * KH, (head + 1) * KH)
            vc = slice(head * VH, (head + 1) * VH)
            out = mixed[rows, vc]
            scale = lax.rsqrt(jnp.mean(out * out, axis=-1, keepdims=True) + HEAD_FLOOR)
            unit = out * scale
            gate_rows = gate[rows, vc]
            sig = jax.nn.sigmoid(gate_rows)
            swish = gate_rows * sig
            grad = grad_gated[rows, vc]
            grad_n = grad * unit
            headnorm_out[...] += jnp.sum(grad_n * swish, axis=0, keepdims=True)
            grad_gate_out[rows, vc] = (
                grad_n * gain_row * sig * (1.0 + gate_rows * (1.0 - sig))
            ).astype(BF)
            grad_unit = grad * gain_row * swish
            grad_mixed = scale * (
                grad_unit - unit * jnp.mean(grad_unit * unit, axis=-1, keepdims=True)
            )
            grad_mixed = grad_mixed.astype(BF)
            grad_mixed_out[rows, vc] = grad_mixed
            adjoint_out[vc, :] = adjoint_out[vc, :] * through[:, kc] + mm(
                grad_mixed, reach[:, kc], 0, 0
            )
        return 0

    lax.fori_loop(0, count, step, 0, unroll=4)


def backward_kernel(
    heads,
    ids_s,
    prev_s,
    ids_c,
    ids_r,
    query,
    key,
    value,
    total_in,
    grad_mixed,
    states,
    adjoint_in,
    grad_query_out,
    grad_key_out,
    grad_value_out,
    grad_decay_out,
    adjoint,
):
    count = key.shape[0] // BLOCK
    adjoint[...] = adjoint_in[...]
    later = lax.broadcasted_iota(jnp.int32, (BLOCK, BLOCK), 0)
    earlier = lax.broadcasted_iota(jnp.int32, (BLOCK, BLOCK), 1)
    upper = tri(BLOCK, False, 2)

    def step(turn, _):
        block = count - 1 - turn
        rows = pl.ds(pl.multiple_of(block * BLOCK, BLOCK), BLOCK)
        last, prev = block_ids(ids_s, prev_s, block)
        ids = ids_c[rows, :]
        linked = (ids == ids_r[pl.ds(block, 1), :]) & (later >= earlier)
        keep = (ids == last).astype(F32)
        alive = (ids == prev).astype(F32) * SCALE
        survive = (last == prev).astype(F32)
        total_all = total_in[rows, :]
        final_all = total_all[BLOCK - 1 : BLOCK, :]
        anchor_all = total_all[BLOCK // 2 : BLOCK // 2 + 1, :]
        for head in range(heads):
            kc = slice(head * KH, (head + 1) * KH)
            vc = slice(head * VH, (head + 1) * VH)
            total = total_all[:, kc]
            final = final_all[:, kc]
            anchor = anchor_all[:, kc]
            query_f = query[rows, kc].astype(F32)
            key_f = key[rows, kc].astype(F32)
            query_grow = SCALE * jnp.exp(total - anchor)
            key_grow = jnp.exp(anchor - total)
            reach_grow = jnp.exp(total) * alive
            tail_grow = jnp.exp(final - total) * keep
            through = survive * jnp.exp(final)
            query_scaled = (query_f * query_grow).astype(BF)
            key_scaled = (key_f * key_grow).astype(BF)
            reach = (query_f * reach_grow).astype(BF)
            tail = (key_f * tail_grow).astype(BF)
            value_rows = value[rows, vc]
            grad = grad_mixed[rows, vc]
            before = states[block, vc, :]
            after = adjoint[vc, :]
            after_b = after.astype(BF)
            scores = mm(query_scaled, key_scaled, 1, 1)
            scores = jnp.where(linked, scores, 0.0).astype(BF)
            grad_scores = mm(grad, value_rows, 1, 1)
            grad_scores = jnp.where(linked, grad_scores, 0.0).astype(BF)
            grad_query_scaled = mm(grad_scores, key_scaled)
            grad_key_scaled = mm(grad_scores, query_scaled, 0, 0)
            grad_reach = mm(grad, before)
            grad_tail = mm(value_rows, after_b)
            grad_query_out[rows, kc] = (
                grad_query_scaled * query_grow + grad_reach * reach_grow
            ).astype(BF)
            grad_key_out[rows, kc] = (grad_key_scaled * key_grow + grad_tail * tail_grow).astype(BF)
            grad_value_out[rows, vc] = (mm(scores, grad, 0, 0) + mm(tail, after_b, 1, 1)).astype(BF)
            tail_part = tail.astype(F32) * grad_tail
            grad_total = (
                query_scaled.astype(F32) * grad_query_scaled
                - key_scaled.astype(F32) * grad_key_scaled
                + reach.astype(F32) * grad_reach
                - tail_part
            )
            grad_final = jnp.sum(tail_part, axis=0, keepdims=True) + through * jnp.sum(
                before.astype(F32) * after, axis=0, keepdims=True
            )
            hi, low = split_hi_lo(grad_total)
            grad_decay_out[rows, kc] = (
                mm(upper, jnp.concatenate([hi, low], axis=0)) + grad_final
            )
            adjoint[vc, :] = after * through + mm(grad, reach, 0, 0)
        return 0

    lax.fori_loop(0, count, step, 0, unroll=2)


def call(kernel, outs, kinds, args, flops, scratch=()):
    spaces = {"s": pltpu.SMEM, "v": pltpu.VMEM}
    shapes = [jax.ShapeDtypeStruct(shape, kind) for shape, kind in outs]
    moved = sum(a.size * a.dtype.itemsize for a in list(args) + shapes)
    return pl.pallas_call(
        kernel,
        out_shape=shapes,
        in_specs=[pl.BlockSpec(memory_space=spaces[kind]) for kind in kinds],
        out_specs=[pl.BlockSpec(memory_space=pltpu.VMEM)] * len(outs),
        scratch_shapes=list(scratch),
        cost_estimate=pl.CostEstimate(flops=flops, bytes_accessed=moved, transcendentals=0),
        compiler_params=pltpu.CompilerParams(vmem_limit_bytes=VMEM_LIMIT),
    )(*args)


def ending_call(ids, prev, ids_col, key, value, decay):
    length, keys = key.shape
    heads = keys // KH
    return call(
        functools.partial(ending_kernel, heads),
        [((length, keys), F32), ((heads * VH, KH), F32), ((1, keys), F32)],
        "ssvvvv",
        (ids, prev, ids_col, key, value, decay),
        8 * 10**9,
    )


def forward_call(ids, prev, ids_col, ids_row, query, key, value, total, gate, gain, state):
    length, keys = key.shape
    heads = keys // KH
    return call(
        functools.partial(forward_kernel, heads),
        [
            ((length, heads * VH), F32),
            ((length, heads * VH), BF),
            ((length // BLOCK, heads * VH, KH), BF),
        ],
        "ssvvvvvvvvv",
        (ids, prev, ids_col, ids_row, query, key, value, total, gate, gain, state),
        20 * 10**9,
        [pltpu.VMEM((heads * VH, KH), F32)],
    )


def back_start_call(ids, prev, ids_col, query, total, gate, gain, mixed, grad_gated):
    length, keys = query.shape
    heads = keys // KH
    return call(
        functools.partial(back_start_kernel, heads),
        [
            ((length, heads * VH), BF),
            ((length, heads * VH), BF),
            ((1, VH), F32),
            ((heads * VH, KH), F32),
        ],
        "ssvvvvvvv",
        (ids, prev, ids_col, query, total, gate, gain, mixed, grad_gated),
        15 * 10**9,
    )


def backward_call(ids, prev, ids_col, ids_row, query, key, value, total, grad, states, adjoint):
    length, keys = key.shape
    heads = keys // KH
    return call(
        functools.partial(backward_kernel, heads),
        [
            ((length, keys), BF),
            ((length, keys), BF),
            ((length, heads * VH), BF),
            ((length, keys), F32),
        ],
        "ssvvvvvvvvv",
        (ids, prev, ids_col, ids_row, query, key, value, total, grad, states, adjoint),
        40 * 10**9,
        [pltpu.VMEM((heads * VH, KH), F32)],
    )


def swap(array, axis, bit):
    count = lax.axis_size(axis)
    return lax.ppermute(array, axis, [(i, i ^ bit) for i in range(count)])


def both(part):
    sent = part.astype(BF)
    return sent.astype(F32) + swap(sent, "tp", 1).astype(F32)


def pick(array, index, axis):
    return lax.dynamic_index_in_dim(array, index, axis, False)


def paired(mine, other, bit, axis):
    low = jnp.where(bit == 0, mine, other)
    high = jnp.where(bit == 0, other, mine)
    return jnp.stack([low, high], axis=axis)


def along_ctx(array):
    place = lax.axis_index("ctx")
    x_bit, y_bit = place % 2, place // 2
    half = array.shape[0] // 2

    def x_first(part):
        row = paired(part, swap(part, "ctx", 1), x_bit, -3)
        whole = paired(row, swap(row, "ctx", 2), y_bit, -4)
        return whole.reshape(*part.shape[:-2], 4, *part.shape[-2:])

    def y_first(part):
        row = paired(part, swap(part, "ctx", 2), y_bit, -3)
        whole = paired(row, swap(row, "ctx", 1), x_bit, -3)
        return whole.reshape(*part.shape[:-2], 4, *part.shape[-2:])

    return jnp.concatenate([x_first(array[:half]), y_first(array[half:])], axis=0)


def gather_rows(shard):
    rows, columns = shard.shape
    count, ctx = lax.axis_size("fsdp"), lax.axis_size("ctx")
    if ctx != 4 or count % 2:
        return lax.all_gather(shard, "fsdp", axis=0, tiled=True)
    part = lax.dynamic_slice_in_dim(shard, lax.axis_index("ctx") * (rows // ctx), rows // ctx, 0)
    if count > 4:
        pieces = lax.all_gather(part, "fsdp", axis=0)
    else:
        place = lax.axis_index("fsdp")
        pieces = jnp.zeros((count, *part.shape), part.dtype)
        pieces = lax.dynamic_update_index_in_dim(pieces, part, place, 0)
        for shift in range(1, count):
            moved = lax.ppermute(part, "fsdp", [(i, (i + shift) % count) for i in range(count)])
            pieces = lax.dynamic_update_index_in_dim(pieces, moved, (place - shift) % count, 0)
    return along_ctx(pieces).reshape(count * rows, columns)


def reduce_rows(grad):
    rows, columns = grad.shape
    count, ctx = lax.axis_size("fsdp"), lax.axis_size("ctx")
    grad = grad.astype(BF)
    if ctx != 4 or count % 2:
        own = lax.psum_scatter(grad, "fsdp", scatter_dimension=0, tiled=True)
        return lax.psum(own, "ctx").astype(F32)
    place = lax.axis_index("ctx")
    x_bit, y_bit = place % 2, place // 2
    size = rows // (count * ctx)
    blocks = grad.reshape(count, 2, 2, size, columns)
    half = count // 2

    def fold(array, bit, step, axis):
        theirs = swap(pick(array, 1 - bit, axis), "ctx", step)
        return (pick(array, bit, axis).astype(F32) + theirs.astype(F32)).astype(BF)

    first = fold(fold(blocks[:half], x_bit, 1, 2), y_bit, 2, 1)
    second = fold(fold(blocks[half:], y_bit, 2, 1), x_bit, 1, 1)
    partial = jnp.concatenate([first, second], axis=0)
    if count > 4:
        own = lax.psum_scatter(partial, "fsdp", scatter_dimension=0, tiled=False)
    else:
        at = lax.axis_index("fsdp")
        total = pick(partial, at, 0).astype(F32)
        for shift in range(1, count):
            sent = pick(partial, (at + shift) % count, 0)
            moved = lax.ppermute(sent, "fsdp", [(i, (i + shift) % count) for i in range(count)])
            total = total + moved.astype(F32)
        own = total.astype(BF)
    halves = own.reshape(2, size // 2, columns)
    whole = along_ctx(halves)
    return jnp.moveaxis(whole, 0, 1).reshape(ctx * size, columns).astype(F32)


def shifted(value, axis, steps):
    count = lax.axis_size(axis)
    initial, last = (max(0, -steps), min(count, count - steps))
    return lax.ppermute(value, axis, [(source, source + steps) for source in range(initial, last)])


def dot(left, right, left_dim=1, right_dim=0):
    return lax.dot_general(
        left, right, (((left_dim,), (right_dim,)), ((), ())), preferred_element_type=F32
    )


def rms_scale(rows):
    return lax.rsqrt(jnp.mean(rows * rows, axis=-1, keepdims=True) + EPSILON)


def norm_back(grad_normed, rows, scale, gain):
    inner_term = gain * grad_normed
    return scale * (
        inner_term - rows * scale * scale * jnp.mean(inner_term * rows, axis=-1, keepdims=True)
    )


def chain(decay, state, order, used):
    out = jnp.zeros_like(state[0])
    for source in order:
        out = jnp.where(used(source), decay[source] * out + state[source].astype(F32), out)
    return out


def body(
    tokens,
    doc_ids,
    prenorm,
    w_query,
    w_key,
    w_value,
    w_outgate,
    w_lowrank,
    w_decay,
    decay_bias,
    headnorm,
    w_output,
    postnorm,
    w_gate,
    w_up,
    w_down,
    cotangent,
):
    keys, values = w_query.shape[1], w_value.shape[1]
    rank, hidden_size = w_lowrank.shape[1], w_gate.shape[1]
    heads = keys // KH
    mixer_size = 2 * keys + 2 * values
    extra = -(rank + 2) % 128
    pad = jnp.zeros((prenorm.shape[0], extra), BF)
    mixer_pack = jnp.concatenate(
        [w_query, w_key, w_value, w_outgate, w_lowrank, prenorm[:, None], postnorm[:, None], pad],
        axis=1,
    )
    mixer_all = gather_rows(mixer_pack)
    mat_output = gather_rows(w_output.T).T
    mat_ffn = gather_rows(jnp.concatenate([w_gate, w_up], axis=1))
    mat_down_t = gather_rows(w_down.T)
    mat_lowrank = mixer_all[:, mixer_size : mixer_size + rank]
    gain_first = mixer_all[:, mixer_size + rank].astype(F32)
    gain_second = mixer_all[:, mixer_size + rank + 1].astype(F32)
    gain_head = headnorm.astype(F32)[None, :]

    place, pieces = lax.axis_index("ctx"), lax.axis_size("ctx")
    ids = doc_ids[0]
    last_id = ids[-1:]
    prev_id = shifted(last_id, "ctx", 1)
    link = (last_id == prev_id).astype(F32)
    ids_col, ids_row = ids[:, None], ids.reshape(-1, BLOCK)

    resid_in = tokens[0].astype(F32)
    scale_one = rms_scale(resid_in)
    normed_one = (resid_in * scale_one * gain_first).astype(BF)
    projected = dot(normed_one, mixer_all)
    query = projected[:, :keys].astype(BF)
    key = projected[:, keys : 2 * keys].astype(BF)
    value = projected[:, 2 * keys : 2 * keys + values].astype(BF)
    gate_pre = projected[:, 2 * keys + values : mixer_size]
    rank_act = projected[:, mixer_size : mixer_size + rank].astype(BF)
    decay_logit = dot(rank_act, w_decay) + decay_bias.astype(F32)
    log_decay = jax.nn.log_sigmoid(decay_logit) / NORMALIZER

    total, ending, decay_sum = ending_call(ids, prev_id, ids_col, key, value, log_decay)
    through = jnp.exp(decay_sum) * link
    through_all = lax.all_gather(through, "ctx")
    ending_all = lax.all_gather(ending, "ctx")
    columns = jnp.repeat(through_all.reshape(pieces, heads, 1, KH), VH, axis=2)
    columns = columns.reshape(pieces, heads * VH, KH)
    incoming = chain(columns, ending_all, range(pieces), lambda source: source < place)
    mixed, gated, states = forward_call(
        ids, prev_id, ids_col, ids_row, query, key, value, total, gate_pre, gain_head, incoming
    )

    resid_mid = resid_in + both(dot(gated, mat_output))
    scale_two = rms_scale(resid_mid)
    normed_two = (resid_mid * scale_two * gain_second).astype(BF)
    acts = dot(normed_two, mat_ffn)
    gate_act, up_act = acts[:, :hidden_size], acts[:, hidden_size:]
    ffn_sig = jax.nn.sigmoid(gate_act)
    silu_act = gate_act * ffn_sig
    hidden = (silu_act * up_act).astype(BF)
    block_out = (resid_mid + both(dot(hidden, mat_down_t, 1, 1))).astype(BF)
    cot = cotangent[0]
    grad_hidden = dot(cot, mat_down_t)
    grad_gate_act = (grad_hidden * up_act * ffn_sig * (1.0 + gate_act * (1.0 - ffn_sig))).astype(BF)
    grad_up_act = (grad_hidden * silu_act).astype(BF)
    grad_acts = jnp.concatenate([grad_gate_act, grad_up_act], axis=1)
    norm_two_grad = both(dot(grad_acts, mat_ffn, 1, 1))
    grad_down = reduce_rows(dot(cot, hidden, 0, 0).astype(BF)).T
    grad_ffn = reduce_rows(dot(normed_two, grad_acts, 0, 0).astype(BF))
    grad_postnorm = jnp.sum(norm_two_grad * resid_mid * scale_two, axis=0)
    grad_mid = cot.astype(F32) + norm_back(norm_two_grad, resid_mid, scale_two, gain_second)
    grad_attn = grad_mid.astype(BF)
    grad_gated = dot(grad_attn, mat_output, 1, 1)
    grad_output = reduce_rows(dot(grad_attn, gated, 0, 0).astype(BF)).T

    grad_mixed, grad_gate_rows, headnorm_part, adjoint = back_start_call(
        ids, prev_id, ids_col, query, total, gate_pre, gain_head, mixed, grad_gated
    )
    adjoint_all = lax.all_gather(adjoint.astype(BF), "ctx")
    adjoint_in = chain(
        columns, adjoint_all, range(pieces - 1, -1, -1), lambda source: source > place
    )
    grad_query, grad_key, grad_value, grad_log_decay = backward_call(
        ids, prev_id, ids_col, ids_row, query, key, value, total, grad_mixed, states, adjoint_in
    )
    grad_logit = (grad_log_decay * jax.nn.sigmoid(-decay_logit) / NORMALIZER).astype(BF)
    grad_decay = dot(rank_act, grad_logit, 0, 0)
    grad_bias = jnp.sum(grad_logit.astype(F32), axis=0, keepdims=True)
    grad_rank = both(dot(grad_logit, w_decay, 1, 1)).astype(BF)
    grad_heads = jnp.concatenate([grad_query, grad_key, grad_value, grad_gate_rows], axis=1)
    grad_mixer = dot(normed_one, grad_heads, 0, 0).astype(BF)
    grad_lowrank = dot(normed_one, grad_rank, 0, 0).astype(BF)
    norm_one_grad = both(dot(grad_heads, mixer_all[:, :mixer_size], 1, 1))
    norm_one_grad = norm_one_grad + dot(grad_rank, mat_lowrank, 1, 1)
    grad_prenorm = jnp.sum(norm_one_grad * resid_in * scale_one, axis=0)
    grad_tokens = (grad_mid + norm_back(norm_one_grad, resid_in, scale_one, gain_first)).astype(BF)
    grad_heads_own = reduce_rows(grad_mixer)
    grad_small = jnp.concatenate(
        [
            grad_lowrank,
            grad_prenorm[:, None].astype(BF),
            grad_postnorm[:, None].astype(BF),
            jnp.zeros((grad_lowrank.shape[0], extra), BF),
        ],
        axis=1,
    )
    small_own = reduce_rows(grad_small)
    sums = lax.psum(
        jnp.concatenate([grad_decay, grad_bias, both(headnorm_part)], axis=0), ("fsdp", "ctx")
    )
    return (
        block_out[None],
        grad_tokens[None],
        small_own[:, rank],
        grad_heads_own[:, :keys],
        grad_heads_own[:, keys : 2 * keys],
        grad_heads_own[:, 2 * keys : 2 * keys + values],
        grad_heads_own[:, 2 * keys + values :],
        small_own[:, :rank],
        sums[:rank],
        sums[rank],
        sums[rank + 1],
        grad_output,
        small_own[:, rank + 1],
        grad_ffn[:, :hidden_size],
        grad_ffn[:, hidden_size:],
        grad_down,
    )


def solution(mesh):
    in_specs = (
        P("fsdp", "ctx", None),
        P("fsdp", "ctx"),
        P("fsdp"),
        P("fsdp", "tp"),
        P("fsdp", "tp"),
        P("fsdp", "tp"),
        P("fsdp", "tp"),
        P("fsdp", None),
        P(None, "tp"),
        P("tp"),
        P(),
        P("tp", "fsdp"),
        P("fsdp"),
        P("fsdp", "tp"),
        P("fsdp", "tp"),
        P("tp", "fsdp"),
        P("fsdp", "ctx", None),
    )
    out_specs = (
        P("fsdp", "ctx", None),
        P("fsdp", "ctx", None),
        P("fsdp"),
        P("fsdp", "tp"),
        P("fsdp", "tp"),
        P("fsdp", "tp"),
        P("fsdp", "tp"),
        P("fsdp", None),
        P(None, "tp"),
        P("tp"),
        P(),
        P("tp", "fsdp"),
        P("fsdp"),
        P("fsdp", "tp"),
        P("fsdp", "tp"),
        P("tp", "fsdp"),
    )
    return jax.shard_map(body, mesh=mesh, in_specs=in_specs, out_specs=out_specs, check_vma=False)
```

```python
import functools

import jax
import jax.numpy as jnp
from jax import lax
from jax.experimental import pallas as pl
from jax.experimental.pallas import tpu as pltpu
from jax.sharding import PartitionSpec as P

KH = 128
VH = 256
BLOCK = 64


EPSILON = 1e-06
HEAD_FLOOR = 1.0
NORMALIZER = 16.0
SCALE = KH ** (-0.5)
BF = jnp.bfloat16
F32 = jnp.float32
VMEM_LIMIT = 50 * 1024 * 1024


def mm(left, right, left_dim=1, right_dim=0):
    return lax.dot_general(
        left, right, (((left_dim,), (right_dim,)), ((), ())), preferred_element_type=F32
    )


def split_hi_lo(array):
    hi = array.astype(BF)
    return hi, (array - hi.astype(F32)).astype(BF)


def tri(rows, inclusive_lower, copies):
    at_row = lax.broadcasted_iota(jnp.int32, (rows, rows), 0)
    at_col = lax.broadcasted_iota(jnp.int32, (rows, rows), 1)
    mask = at_row >= at_col if inclusive_lower else at_row <= at_col
    square = mask.astype(F32).astype(BF)
    return jnp.concatenate([square] * copies, axis=1)


def block_ids(ids_smem, prev_smem, block):
    last = ids_smem[block * BLOCK + BLOCK - 1]
    before = ids_smem[jnp.maximum(block * BLOCK - 1, 0)]
    prev = jnp.where(block == 0, prev_smem[0], before)
    return last, prev


def ending_kernel(heads, ids_s, prev_s, ids_c, key, value, decay, total_out, state_out, sum_out):
    count = key.shape[0] // BLOCK
    state_out[...] = jnp.zeros_like(state_out)
    sum_out[...] = jnp.zeros_like(sum_out)
    lower = tri(BLOCK, True, 3)

    def step(block, _):
        rows = pl.ds(pl.multiple_of(block * BLOCK, BLOCK), BLOCK)
        last, prev = block_ids(ids_s, prev_s, block)
        keep = (ids_c[rows, :] == last).astype(F32)
        survive = (last == prev).astype(F32)
        decay_rows = decay[rows, :]
        hi, rest = decay_rows.astype(BF), decay_rows
        rest = rest - hi.astype(F32)
        mid, low = split_hi_lo(rest)
        total = mm(lower, jnp.concatenate([hi, mid, low], axis=0))
        total_out[rows, :] = total
        final = total[BLOCK - 1 : BLOCK, :]
        sum_out[...] += final
        tail = (key[rows, :].astype(F32) * jnp.exp(final - total) * keep).astype(BF)
        through = survive * jnp.exp(final)
        for head in range(heads):
            kc = slice(head * KH, (head + 1) * KH)
            vc = slice(head * VH, (head + 1) * VH)
            fresh = mm(value[rows, vc], tail[:, kc], 0, 0)
            state_out[vc, :] = state_out[vc, :] * through[:, kc] + fresh
        return 0

    lax.fori_loop(0, count, step, 0, unroll=4)


def forward_kernel(
    heads,
    ids_s,
    prev_s,
    ids_c,
    ids_r,
    query,
    key,
    value,
    total_in,
    gate,
    gain,
    state_in,
    mixed_out,
    gated_out,
    states_out,
    state,
):
    count = key.shape[0] // BLOCK
    state[...] = state_in[...]
    later = lax.broadcasted_iota(jnp.int32, (BLOCK, BLOCK), 0)
    earlier = lax.broadcasted_iota(jnp.int32, (BLOCK, BLOCK), 1)

    def step(block, _):
        rows = pl.ds(pl.multiple_of(block * BLOCK, BLOCK), BLOCK)
        last, prev = block_ids(ids_s, prev_s, block)
        ids = ids_c[rows, :]
        linked = (ids == ids_r[pl.ds(block, 1), :]) & (later >= earlier)
        keep = (ids == last).astype(F32)
        alive = (ids == prev).astype(F32) * SCALE
        survive = (last == prev).astype(F32)
        total = total_in[rows, :]
        final = total[BLOCK - 1 : BLOCK, :]
        anchor = total[BLOCK // 2 : BLOCK // 2 + 1, :]
        query_f = query[rows, :].astype(F32)
        key_f = key[rows, :].astype(F32)
        query_scaled = (query_f * SCALE * jnp.exp(total - anchor)).astype(BF)
        key_scaled = (key_f * jnp.exp(anchor - total)).astype(BF)
        reach = (query_f * jnp.exp(total) * alive).astype(BF)
        tail = (key_f * jnp.exp(final - total) * keep).astype(BF)
        through = survive * jnp.exp(final)
        for head in range(heads):
            kc = slice(head * KH, (head + 1) * KH)
            vc = slice(head * VH, (head + 1) * VH)
            value_rows = value[rows, vc]
            scores = mm(query_scaled[:, kc], key_scaled[:, kc], 1, 1)
            scores = jnp.where(linked, scores, 0.0).astype(BF)
            now = state[vc, :]
            now_b = now.astype(BF)
            states_out[block, vc, :] = now_b
            out = mm(scores, value_rows) + mm(reach[:, kc], now_b, 1, 1)
            mixed_out[rows, vc] = out
            state[vc, :] = now * through[:, kc] + mm(value_rows, tail[:, kc], 0, 0)
            unit = out * lax.rsqrt(jnp.mean(out * out, axis=-1, keepdims=True) + HEAD_FLOOR)
            gate_rows = gate[rows, vc]
            swish = gate_rows * jax.nn.sigmoid(gate_rows)
            gated_out[rows, vc] = (unit * gain[...] * swish).astype(BF)
        return 0

    lax.fori_loop(0, count, step, 0, unroll=4)


def back_start_kernel(
    heads,
    ids_s,
    prev_s,
    ids_c,
    query,
    total_in,
    gate,
    gain,
    mixed,
    grad_gated,
    grad_mixed_out,
    grad_gate_out,
    headnorm_out,
    adjoint_out,
):
    count = query.shape[0] // BLOCK
    adjoint_out[...] = jnp.zeros_like(adjoint_out)
    headnorm_out[...] = jnp.zeros_like(headnorm_out)

    def step(turn, _):
        block = count - 1 - turn
        rows = pl.ds(pl.multiple_of(block * BLOCK, BLOCK), BLOCK)
        last, prev = block_ids(ids_s, prev_s, block)
        alive = (ids_c[rows, :] == prev).astype(F32) * SCALE
        survive = (last == prev).astype(F32)
        total = total_in[rows, :]
        final = total[BLOCK - 1 : BLOCK, :]
        reach = (query[rows, :].astype(F32) * jnp.exp(total) * alive).astype(BF)
        through = survive * jnp.exp(final)
        gain_row = gain[...]
        for head in range(heads):
            kc = slice(head * KH, (head + 1) * KH)
            vc = slice(head * VH, (head + 1) * VH)
            out = mixed[rows, vc]
            scale = lax.rsqrt(jnp.mean(out * out, axis=-1, keepdims=True) + HEAD_FLOOR)
            unit = out * scale
            gate_rows = gate[rows, vc]
            sig = jax.nn.sigmoid(gate_rows)
            swish = gate_rows * sig
            grad = grad_gated[rows, vc]
            grad_n = grad * unit
            headnorm_out[...] += jnp.sum(grad_n * swish, axis=0, keepdims=True)
            grad_gate_out[rows, vc] = (
                grad_n * gain_row * sig * (1.0 + gate_rows * (1.0 - sig))
            ).astype(BF)
            grad_unit = grad * gain_row * swish
            grad_mixed = scale * (
                grad_unit - unit * jnp.mean(grad_unit * unit, axis=-1, keepdims=True)
            )
            grad_mixed = grad_mixed.astype(BF)
            grad_mixed_out[rows, vc] = grad_mixed
            adjoint_out[vc, :] = adjoint_out[vc, :] * through[:, kc] + mm(
                grad_mixed, reach[:, kc], 0, 0
            )
        return 0

    lax.fori_loop(0, count, step, 0, unroll=4)


def backward_kernel(
    heads,
    ids_s,
    prev_s,
    ids_c,
    ids_r,
    query,
    key,
    value,
    total_in,
    grad_mixed,
    states,
    adjoint_in,
    grad_query_out,
    grad_key_out,
    grad_value_out,
    grad_decay_out,
    adjoint,
):
    count = key.shape[0] // BLOCK
    adjoint[...] = adjoint_in[...]
    later = lax.broadcasted_iota(jnp.int32, (BLOCK, BLOCK), 0)
    earlier = lax.broadcasted_iota(jnp.int32, (BLOCK, BLOCK), 1)
    upper = tri(BLOCK, False, 2)

    def step(turn, _):
        block = count - 1 - turn
        rows = pl.ds(pl.multiple_of(block * BLOCK, BLOCK), BLOCK)
        last, prev = block_ids(ids_s, prev_s, block)
        ids = ids_c[rows, :]
        linked = (ids == ids_r[pl.ds(block, 1), :]) & (later >= earlier)
        keep = (ids == last).astype(F32)
        alive = (ids == prev).astype(F32) * SCALE
        survive = (last == prev).astype(F32)
        total_all = total_in[rows, :]
        final_all = total_all[BLOCK - 1 : BLOCK, :]
        anchor_all = total_all[BLOCK // 2 : BLOCK // 2 + 1, :]
        for head in range(heads):
            kc = slice(head * KH, (head + 1) * KH)
            vc = slice(head * VH, (head + 1) * VH)
            total = total_all[:, kc]
            final = final_all[:, kc]
            anchor = anchor_all[:, kc]
            query_f = query[rows, kc].astype(F32)
            key_f = key[rows, kc].astype(F32)
            query_grow = SCALE * jnp.exp(total - anchor)
            key_grow = jnp.exp(anchor - total)
            reach_grow = jnp.exp(total) * alive
            tail_grow = jnp.exp(final - total) * keep
            through = survive * jnp.exp(final)
            query_scaled = (query_f * query_grow).astype(BF)
            key_scaled = (key_f * key_grow).astype(BF)
            reach = (query_f * reach_grow).astype(BF)
            tail = (key_f * tail_grow).astype(BF)
            value_rows = value[rows, vc]
            grad = grad_mixed[rows, vc]
            before = states[block, vc, :]
            after = adjoint[vc, :]
            after_b = after.astype(BF)
            scores = mm(query_scaled, key_scaled, 1, 1)
            scores = jnp.where(linked, scores, 0.0).astype(BF)
            grad_scores = mm(grad, value_rows, 1, 1)
            grad_scores = jnp.where(linked, grad_scores, 0.0).astype(BF)
            grad_query_scaled = mm(grad_scores, key_scaled)
            grad_key_scaled = mm(grad_scores, query_scaled, 0, 0)
            grad_reach = mm(grad, before)
            grad_tail = mm(value_rows, after_b)
            grad_query_out[rows, kc] = (
                grad_query_scaled * query_grow + grad_reach * reach_grow
            ).astype(BF)
            grad_key_out[rows, kc] = (grad_key_scaled * key_grow + grad_tail * tail_grow).astype(BF)
            grad_value_out[rows, vc] = (mm(scores, grad, 0, 0) + mm(tail, after_b, 1, 1)).astype(BF)
            tail_part = tail.astype(F32) * grad_tail
            grad_total = (
                query_scaled.astype(F32) * grad_query_scaled
                - key_scaled.astype(F32) * grad_key_scaled
                + reach.astype(F32) * grad_reach
                - tail_part
            )
            grad_final = jnp.sum(tail_part, axis=0, keepdims=True) + through * jnp.sum(
                before.astype(F32) * after, axis=0, keepdims=True
            )
            hi, low = split_hi_lo(grad_total)
            grad_decay_out[rows, kc] = (
                mm(upper, jnp.concatenate([hi, low], axis=0)) + grad_final
            )
            adjoint[vc, :] = after * through + mm(grad, reach, 0, 0)
        return 0

    lax.fori_loop(0, count, step, 0, unroll=2)


def call(kernel, outs, kinds, args, flops, scratch=()):
    spaces = {"s": pltpu.SMEM, "v": pltpu.VMEM}
    shapes = [jax.ShapeDtypeStruct(shape, kind) for shape, kind in outs]
    moved = sum(a.size * a.dtype.itemsize for a in list(args) + shapes)
    return pl.pallas_call(
        kernel,
        out_shape=shapes,
        in_specs=[pl.BlockSpec(memory_space=spaces[kind]) for kind in kinds],
        out_specs=[pl.BlockSpec(memory_space=pltpu.VMEM)] * len(outs),
        scratch_shapes=list(scratch),
        cost_estimate=pl.CostEstimate(flops=flops, bytes_accessed=moved, transcendentals=0),
        compiler_params=pltpu.CompilerParams(vmem_limit_bytes=VMEM_LIMIT),
    )(*args)


def ending_call(ids, prev, ids_col, key, value, decay):
    length, keys = key.shape
    heads = keys // KH
    return call(
        functools.partial(ending_kernel, heads),
        [((length, keys), F32), ((heads * VH, KH), F32), ((1, keys), F32)],
        "ssvvvv",
        (ids, prev, ids_col, key, value, decay),
        8 * 10**9,
    )


def forward_call(ids, prev, ids_col, ids_row, query, key, value, total, gate, gain, state):
    length, keys = key.shape
    heads = keys // KH
    return call(
        functools.partial(forward_kernel, heads),
        [
            ((length, heads * VH), F32),
            ((length, heads * VH), BF),
            ((length // BLOCK, heads * VH, KH), BF),
        ],
        "ssvvvvvvvvv",
        (ids, prev, ids_col, ids_row, query, key, value, total, gate, gain, state),
        20 * 10**9,
        [pltpu.VMEM((heads * VH, KH), F32)],
    )


def back_start_call(ids, prev, ids_col, query, total, gate, gain, mixed, grad_gated):
    length, keys = query.shape
    heads = keys // KH
    return call(
        functools.partial(back_start_kernel, heads),
        [
            ((length, heads * VH), BF),
            ((length, heads * VH), BF),
            ((1, VH), F32),
            ((heads * VH, KH), F32),
        ],
        "ssvvvvvvv",
        (ids, prev, ids_col, query, total, gate, gain, mixed, grad_gated),
        15 * 10**9,
    )


def backward_call(ids, prev, ids_col, ids_row, query, key, value, total, grad, states, adjoint):
    length, keys = key.shape
    heads = keys // KH
    return call(
        functools.partial(backward_kernel, heads),
        [
            ((length, keys), BF),
            ((length, keys), BF),
            ((length, heads * VH), BF),
            ((length, keys), F32),
        ],
        "ssvvvvvvvvv",
        (ids, prev, ids_col, ids_row, query, key, value, total, grad, states, adjoint),
        40 * 10**9,
        [pltpu.VMEM((heads * VH, KH), F32)],
    )


def swap(array, axis, bit):
    count = lax.axis_size(axis)
    return lax.ppermute(array, axis, [(i, i ^ bit) for i in range(count)])


def both(part):
    sent = part.astype(BF)
    return sent.astype(F32) + swap(sent, "tp", 1).astype(F32)


def pick(array, index, axis):
    return lax.dynamic_index_in_dim(array, index, axis, False)


def paired(mine, other, bit, axis):
    low = jnp.where(bit == 0, mine, other)
    high = jnp.where(bit == 0, other, mine)
    return jnp.stack([low, high], axis=axis)


def along_ctx(array):
    place = lax.axis_index("ctx")
    x_bit, y_bit = place % 2, place // 2
    half = array.shape[0] // 2

    def x_first(part):
        row = paired(part, swap(part, "ctx", 1), x_bit, -3)
        whole = paired(row, swap(row, "ctx", 2), y_bit, -4)
        return whole.reshape(*part.shape[:-2], 4, *part.shape[-2:])

    def y_first(part):
        row = paired(part, swap(part, "ctx", 2), y_bit, -3)
        whole = paired(row, swap(row, "ctx", 1), x_bit, -3)
        return whole.reshape(*part.shape[:-2], 4, *part.shape[-2:])

    return jnp.concatenate([x_first(array[:half]), y_first(array[half:])], axis=0)


def after(array, done):
    return array if done is None else lax.optimization_barrier((array, done))[0]


def gather_rows(shard, done=None):
    rows, columns = shard.shape
    count, ctx = lax.axis_size("fsdp"), lax.axis_size("ctx")
    if ctx != 4 or count % 2:
        return lax.all_gather(shard, "fsdp", axis=0, tiled=True), None
    part = lax.dynamic_slice_in_dim(shard, lax.axis_index("ctx") * (rows // ctx), rows // ctx, 0)
    part = after(part, done)
    if count > 4:
        pieces = lax.all_gather(part, "fsdp", axis=0)
    else:
        place = lax.axis_index("fsdp")
        pieces = jnp.zeros((count, *part.shape), part.dtype)
        pieces = lax.dynamic_update_index_in_dim(pieces, part, place, 0)
        for shift in range(1, count):
            moved = lax.ppermute(part, "fsdp", [(i, (i + shift) % count) for i in range(count)])
            pieces = lax.dynamic_update_index_in_dim(pieces, moved, (place - shift) % count, 0)
    return along_ctx(pieces).reshape(count * rows, columns), pieces


def reduce_rows(grad, done=(None, None)):
    rows, columns = grad.shape
    count, ctx = lax.axis_size("fsdp"), lax.axis_size("ctx")
    grad = grad.astype(BF)
    if ctx != 4 or count % 2:
        own = lax.psum_scatter(grad, "fsdp", scatter_dimension=0, tiled=True)
        return lax.psum(own, "ctx").astype(F32)
    place = lax.axis_index("ctx")
    x_bit, y_bit = place % 2, place // 2
    size = rows // (count * ctx)
    blocks = grad.reshape(count, 2, 2, size, columns)
    half = count // 2

    def fold(array, bit, step, axis, late):
        theirs = after(swap(pick(array, 1 - bit, axis), "ctx", step), late)
        return (pick(array, bit, axis).astype(F32) + theirs.astype(F32)).astype(BF)

    first = fold(fold(blocks[:half], x_bit, 1, 2, done[0]), y_bit, 2, 1, done[1])
    second = fold(fold(blocks[half:], y_bit, 2, 1, done[0]), x_bit, 1, 1, done[1])
    partial = jnp.concatenate([first, second], axis=0)
    if count > 4:
        own = lax.psum_scatter(partial, "fsdp", scatter_dimension=0, tiled=False)
    else:
        at = lax.axis_index("fsdp")
        total = pick(partial, at, 0).astype(F32)
        for shift in range(1, count):
            sent = pick(partial, (at + shift) % count, 0)
            moved = lax.ppermute(sent, "fsdp", [(i, (i + shift) % count) for i in range(count)])
            total = total + moved.astype(F32)
        own = total.astype(BF)
    halves = own.reshape(2, size // 2, columns)
    whole = along_ctx(halves)
    return jnp.moveaxis(whole, 0, 1).reshape(ctx * size, columns).astype(F32)


def shifted(value, axis, steps):
    count = lax.axis_size(axis)
    initial, last = (max(0, -steps), min(count, count - steps))
    return lax.ppermute(value, axis, [(source, source + steps) for source in range(initial, last)])


def dot(left, right, left_dim=1, right_dim=0):
    return lax.dot_general(
        left, right, (((left_dim,), (right_dim,)), ((), ())), preferred_element_type=F32
    )


def rms_scale(rows):
    return lax.rsqrt(jnp.mean(rows * rows, axis=-1, keepdims=True) + EPSILON)


def norm_back(grad_normed, rows, scale, gain):
    inner_term = gain * grad_normed
    return scale * (
        inner_term - rows * scale * scale * jnp.mean(inner_term * rows, axis=-1, keepdims=True)
    )


def carried(decay, state, step):
    heads = state.shape[0] // VH
    packed = jnp.concatenate([state, decay.reshape(heads, KH)], axis=0).astype(BF)
    out = jnp.zeros_like(state)
    moved = [shifted(packed, "ctx", step * far) for far in range(1, lax.axis_size("ctx"))]
    for piece in reversed(moved):
        piece = piece.astype(F32)
        grown = jnp.repeat(piece[heads * VH :], VH, axis=0)
        out = grown * out + piece[: heads * VH]
    return out


def sum_all(array):
    for axis in ("ctx", "fsdp"):
        count, bit = lax.axis_size(axis), 1
        if count & (count - 1):
            array = lax.psum(array, axis)
            continue
        while bit < count:
            array = array + swap(array, axis, bit)
            bit *= 2
    return array


def body(
    tokens,
    doc_ids,
    prenorm,
    w_query,
    w_key,
    w_value,
    w_outgate,
    w_lowrank,
    w_decay,
    decay_bias,
    headnorm,
    w_output,
    postnorm,
    w_gate,
    w_up,
    w_down,
    cotangent,
):
    keys, values = w_query.shape[1], w_value.shape[1]
    rank, hidden_size = w_lowrank.shape[1], w_gate.shape[1]
    heads = keys // KH
    mixer_size = 2 * keys + 2 * values
    extra = -(rank + 2) % 128
    pad = jnp.zeros((prenorm.shape[0], extra), BF)
    mixer_pack = jnp.concatenate(
        [w_query, w_key, w_value, w_outgate, w_lowrank, prenorm[:, None], postnorm[:, None], pad],
        axis=1,
    )
    mixer_all, pieces = gather_rows(mixer_pack)
    ffn_pack = jnp.concatenate([w_gate, w_up, w_down.T, w_output.T], axis=1)
    ffn_all, _ = gather_rows(ffn_pack, pieces)
    mat_ffn = ffn_all[:, : 2 * hidden_size]
    mat_down_t = ffn_all[:, 2 * hidden_size : 3 * hidden_size]
    mat_output_t = ffn_all[:, 3 * hidden_size :]
    mat_lowrank = mixer_all[:, mixer_size : mixer_size + rank]
    gain_first = mixer_all[:, mixer_size + rank].astype(F32)
    gain_second = mixer_all[:, mixer_size + rank + 1].astype(F32)
    gain_head = headnorm.astype(F32)[None, :]

    ids = doc_ids[0]
    last_id = ids[-1:]
    prev_id = shifted(last_id, "ctx", 1)
    link = (last_id == prev_id).astype(F32)
    ids_col, ids_row = ids[:, None], ids.reshape(-1, BLOCK)

    resid_in = tokens[0].astype(F32)
    scale_one = rms_scale(resid_in)
    normed_one = (resid_in * scale_one * gain_first).astype(BF)
    projected = dot(normed_one, mixer_all)
    query = projected[:, :keys].astype(BF)
    key = projected[:, keys : 2 * keys].astype(BF)
    value = projected[:, 2 * keys : 2 * keys + values].astype(BF)
    gate_pre = projected[:, 2 * keys + values : mixer_size]
    rank_act = projected[:, mixer_size : mixer_size + rank].astype(BF)
    decay_logit = dot(rank_act, w_decay) + decay_bias.astype(F32)
    log_decay = jax.nn.log_sigmoid(decay_logit) / NORMALIZER

    total, ending, decay_sum = ending_call(ids, prev_id, ids_col, key, value, log_decay)
    through = jnp.exp(decay_sum) * link
    incoming = carried(through, ending, 1)
    mixed, gated, states = forward_call(
        ids, prev_id, ids_col, ids_row, query, key, value, total, gate_pre, gain_head, incoming
    )

    resid_mid = resid_in + both(dot(gated, mat_output_t, 1, 1))
    scale_two = rms_scale(resid_mid)
    normed_two = (resid_mid * scale_two * gain_second).astype(BF)
    acts = dot(normed_two, mat_ffn)
    gate_act, up_act = acts[:, :hidden_size], acts[:, hidden_size:]
    ffn_sig = jax.nn.sigmoid(gate_act)
    silu_act = gate_act * ffn_sig
    hidden = (silu_act * up_act).astype(BF)
    block_out = (resid_mid + both(dot(hidden, mat_down_t, 1, 1))).astype(BF)
    cot = cotangent[0]
    grad_hidden = dot(cot, mat_down_t)
    grad_gate_act = (grad_hidden * up_act * ffn_sig * (1.0 + gate_act * (1.0 - ffn_sig))).astype(BF)
    grad_up_act = (grad_hidden * silu_act).astype(BF)
    grad_acts = jnp.concatenate([grad_gate_act, grad_up_act], axis=1)
    norm_two_grad = both(dot(grad_acts, mat_ffn, 1, 1))
    grad_wide = jnp.concatenate(
        [dot(normed_two, grad_acts, 0, 0).astype(BF), dot(cot, hidden, 0, 0).astype(BF)], axis=1
    )
    grad_wide = after(grad_wide, norm_two_grad)
    grad_postnorm = jnp.sum(norm_two_grad * resid_mid * scale_two, axis=0)
    grad_mid = cot.astype(F32) + norm_back(norm_two_grad, resid_mid, scale_two, gain_second)
    grad_attn = grad_mid.astype(BF)
    grad_gated = dot(grad_attn, mat_output_t)

    grad_mixed, grad_gate_rows, headnorm_part, adjoint = back_start_call(
        ids, prev_id, ids_col, query, total, gate_pre, gain_head, mixed, grad_gated
    )
    adjoint_in = carried(through, adjoint, -1)
    grad_query, grad_key, grad_value, grad_log_decay = backward_call(
        ids, prev_id, ids_col, ids_row, query, key, value, total, grad_mixed, states, adjoint_in
    )
    grad_logit = (grad_log_decay * jax.nn.sigmoid(-decay_logit) / NORMALIZER).astype(BF)
    grad_decay = dot(rank_act, grad_logit, 0, 0)
    grad_bias = jnp.sum(grad_logit.astype(F32), axis=0, keepdims=True)
    grad_rank = both(dot(grad_logit, w_decay, 1, 1)).astype(BF)
    grad_heads = jnp.concatenate([grad_query, grad_key, grad_value, grad_gate_rows], axis=1)
    grad_mixer = jnp.concatenate(
        [dot(normed_one, grad_heads, 0, 0).astype(BF), dot(grad_attn, gated, 0, 0).astype(BF)],
        axis=1,
    )
    grad_lowrank = dot(grad_rank, normed_one, 0, 0)
    norm_one_grad = both(dot(grad_heads, mixer_all[:, :mixer_size], 1, 1))
    norm_one_grad = norm_one_grad + dot(grad_rank, mat_lowrank, 1, 1)
    grad_prenorm = jnp.sum(norm_one_grad * resid_in * scale_one, axis=0)
    grad_tokens = (grad_mid + norm_back(norm_one_grad, resid_in, scale_one, gain_first)).astype(BF)
    wide_own = reduce_rows(grad_wide, (grad_mixed, grad_query))
    heads_own = reduce_rows(grad_mixer)
    width = tokens.shape[2]
    tall = jnp.concatenate([grad_lowrank, grad_prenorm[None], grad_postnorm[None]], axis=0)
    narrow = jnp.concatenate([grad_decay, grad_bias, both(headnorm_part)], axis=0)
    sums = sum_all(jnp.concatenate([tall, narrow], axis=1))
    rows = prenorm.shape[0]
    small_own = lax.dynamic_slice_in_dim(sums, lax.axis_index("fsdp") * rows, rows, 1)
    narrow = sums[:, width:]
    return (
        block_out[None],
        grad_tokens[None],
        small_own[rank],
        heads_own[:, :keys],
        heads_own[:, keys : 2 * keys],
        heads_own[:, 2 * keys : 2 * keys + values],
        heads_own[:, 2 * keys + values : mixer_size],
        small_own[:rank].T,
        narrow[:rank],
        narrow[rank],
        narrow[rank + 1],
        heads_own[:, mixer_size:].T,
        small_own[rank + 1],
        wide_own[:, :hidden_size],
        wide_own[:, hidden_size : 2 * hidden_size],
        wide_own[:, 2 * hidden_size :].T,
    )


def solution(mesh):
    in_specs = (
        P("fsdp", "ctx", None),
        P("fsdp", "ctx"),
        P("fsdp"),
        P("fsdp", "tp"),
        P("fsdp", "tp"),
        P("fsdp", "tp"),
        P("fsdp", "tp"),
        P("fsdp", None),
        P(None, "tp"),
        P("tp"),
        P(),
        P("tp", "fsdp"),
        P("fsdp"),
        P("fsdp", "tp"),
        P("fsdp", "tp"),
        P("tp", "fsdp"),
        P("fsdp", "ctx", None),
    )
    out_specs = (
        P("fsdp", "ctx", None),
        P("fsdp", "ctx", None),
        P("fsdp"),
        P("fsdp", "tp"),
        P("fsdp", "tp"),
        P("fsdp", "tp"),
        P("fsdp", "tp"),
        P("fsdp", None),
        P(None, "tp"),
        P("tp"),
        P(),
        P("tp", "fsdp"),
        P("fsdp"),
        P("fsdp", "tp"),
        P("fsdp", "tp"),
        P("tp", "fsdp"),
    )
    return jax.shard_map(body, mesh=mesh, in_specs=in_specs, out_specs=out_specs, check_vma=False)
```

```python
import functools

import jax
import jax.numpy as jnp
from jax import lax
from jax.experimental import pallas as pl
from jax.experimental.pallas import tpu as pltpu
from jax.sharding import PartitionSpec as P

KH = 128
VH = 256
BLOCK = 64


EPSILON = 1e-06
HEAD_FLOOR = 1.0
NORMALIZER = 16.0
SCALE = KH ** (-0.5)
BF = jnp.bfloat16
F32 = jnp.float32
VMEM_LIMIT = 50 * 1024 * 1024


def mm(left, right, left_dim=1, right_dim=0):
    return lax.dot_general(
        left, right, (((left_dim,), (right_dim,)), ((), ())), preferred_element_type=F32
    )


def split_hi_lo(array):
    hi = array.astype(BF)
    return hi, (array - hi.astype(F32)).astype(BF)


def tri(rows, inclusive_lower, copies):
    at_row = lax.broadcasted_iota(jnp.int32, (rows, rows), 0)
    at_col = lax.broadcasted_iota(jnp.int32, (rows, rows), 1)
    mask = at_row >= at_col if inclusive_lower else at_row <= at_col
    square = mask.astype(F32).astype(BF)
    return jnp.concatenate([square] * copies, axis=1)


def block_ids(ids_smem, prev_smem, block):
    last = ids_smem[block * BLOCK + BLOCK - 1]
    before = ids_smem[jnp.maximum(block * BLOCK - 1, 0)]
    prev = jnp.where(block == 0, prev_smem[0], before)
    return last, prev


def ending_kernel(heads, ids_s, prev_s, ids_c, key, value, decay, total_out, state_out, sum_out):
    count = key.shape[0] // BLOCK
    state_out[...] = jnp.zeros_like(state_out)
    sum_out[...] = jnp.zeros_like(sum_out)
    lower = tri(BLOCK, True, 3)

    def step(block, _):
        rows = pl.ds(pl.multiple_of(block * BLOCK, BLOCK), BLOCK)
        last, prev = block_ids(ids_s, prev_s, block)
        keep = (ids_c[rows, :] == last).astype(F32)
        survive = (last == prev).astype(F32)
        decay_rows = decay[rows, :]
        hi, rest = decay_rows.astype(BF), decay_rows
        rest = rest - hi.astype(F32)
        mid, low = split_hi_lo(rest)
        total = mm(lower, jnp.concatenate([hi, mid, low], axis=0))
        total_out[rows, :] = total
        final = total[BLOCK - 1 : BLOCK, :]
        sum_out[...] += final
        tail = (key[rows, :].astype(F32) * jnp.exp(final - total) * keep).astype(BF)
        through = survive * jnp.exp(final)
        for head in range(heads):
            kc = slice(head * KH, (head + 1) * KH)
            vc = slice(head * VH, (head + 1) * VH)
            fresh = mm(value[rows, vc], tail[:, kc], 0, 0)
            state_out[vc, :] = state_out[vc, :] * through[:, kc] + fresh
        return 0

    lax.fori_loop(0, count, step, 0, unroll=4)


def forward_kernel(
    heads,
    ids_s,
    prev_s,
    ids_c,
    ids_r,
    query,
    key,
    value,
    total_in,
    gate,
    gain,
    state_in,
    mixed_out,
    gated_out,
    states_out,
    state,
):
    count = key.shape[0] // BLOCK
    state[...] = state_in[...]
    later = lax.broadcasted_iota(jnp.int32, (BLOCK, BLOCK), 0)
    earlier = lax.broadcasted_iota(jnp.int32, (BLOCK, BLOCK), 1)

    def step(block, _):
        rows = pl.ds(pl.multiple_of(block * BLOCK, BLOCK), BLOCK)
        last, prev = block_ids(ids_s, prev_s, block)
        ids = ids_c[rows, :]
        linked = (ids == ids_r[pl.ds(block, 1), :]) & (later >= earlier)
        keep = (ids == last).astype(F32)
        alive = (ids == prev).astype(F32) * SCALE
        survive = (last == prev).astype(F32)
        total = total_in[rows, :]
        final = total[BLOCK - 1 : BLOCK, :]
        anchor = total[BLOCK // 2 : BLOCK // 2 + 1, :]
        query_f = query[rows, :].astype(F32)
        key_f = key[rows, :].astype(F32)
        query_scaled = (query_f * SCALE * jnp.exp(total - anchor)).astype(BF)
        key_scaled = (key_f * jnp.exp(anchor - total)).astype(BF)
        reach = (query_f * jnp.exp(total) * alive).astype(BF)
        tail = (key_f * jnp.exp(final - total) * keep).astype(BF)
        through = survive * jnp.exp(final)
        for head in range(heads):
            kc = slice(head * KH, (head + 1) * KH)
            vc = slice(head * VH, (head + 1) * VH)
            value_rows = value[rows, vc]
            scores = mm(query_scaled[:, kc], key_scaled[:, kc], 1, 1)
            scores = jnp.where(linked, scores, 0.0).astype(BF)
            now = state[vc, :]
            now_b = now.astype(BF)
            states_out[block, vc, :] = now_b
            out = mm(scores, value_rows) + mm(reach[:, kc], now_b, 1, 1)
            mixed_out[rows, vc] = out
            state[vc, :] = now * through[:, kc] + mm(value_rows, tail[:, kc], 0, 0)
            unit = out * lax.rsqrt(jnp.mean(out * out, axis=-1, keepdims=True) + HEAD_FLOOR)
            gate_rows = gate[rows, vc]
            swish = gate_rows * jax.nn.sigmoid(gate_rows)
            gated_out[rows, vc] = (unit * gain[...] * swish).astype(BF)
        return 0

    lax.fori_loop(0, count, step, 0, unroll=4)


def back_start_kernel(
    heads,
    ids_s,
    prev_s,
    ids_c,
    query,
    total_in,
    gate,
    gain,
    mixed,
    grad_gated,
    grad_mixed_out,
    grad_gate_out,
    headnorm_out,
    adjoint_out,
):
    count = query.shape[0] // BLOCK
    adjoint_out[...] = jnp.zeros_like(adjoint_out)
    headnorm_out[...] = jnp.zeros_like(headnorm_out)

    def step(turn, _):
        block = count - 1 - turn
        rows = pl.ds(pl.multiple_of(block * BLOCK, BLOCK), BLOCK)
        last, prev = block_ids(ids_s, prev_s, block)
        alive = (ids_c[rows, :] == prev).astype(F32) * SCALE
        survive = (last == prev).astype(F32)
        total = total_in[rows, :]
        final = total[BLOCK - 1 : BLOCK, :]
        reach = (query[rows, :].astype(F32) * jnp.exp(total) * alive).astype(BF)
        through = survive * jnp.exp(final)
        gain_row = gain[...]
        for head in range(heads):
            kc = slice(head * KH, (head + 1) * KH)
            vc = slice(head * VH, (head + 1) * VH)
            out = mixed[rows, vc]
            scale = lax.rsqrt(jnp.mean(out * out, axis=-1, keepdims=True) + HEAD_FLOOR)
            unit = out * scale
            gate_rows = gate[rows, vc]
            sig = jax.nn.sigmoid(gate_rows)
            swish = gate_rows * sig
            grad = grad_gated[rows, vc]
            grad_n = grad * unit
            headnorm_out[...] += jnp.sum(grad_n * swish, axis=0, keepdims=True)
            grad_gate_out[rows, vc] = (
                grad_n * gain_row * sig * (1.0 + gate_rows * (1.0 - sig))
            ).astype(BF)
            grad_unit = grad * gain_row * swish
            grad_mixed = scale * (
                grad_unit - unit * jnp.mean(grad_unit * unit, axis=-1, keepdims=True)
            )
            grad_mixed = grad_mixed.astype(BF)
            grad_mixed_out[rows, vc] = grad_mixed
            adjoint_out[vc, :] = adjoint_out[vc, :] * through[:, kc] + mm(
                grad_mixed, reach[:, kc], 0, 0
            )
        return 0

    lax.fori_loop(0, count, step, 0, unroll=4)


def backward_kernel(
    heads,
    ids_s,
    prev_s,
    ids_c,
    ids_r,
    query,
    key,
    value,
    total_in,
    grad_mixed,
    states,
    adjoint_in,
    grad_query_out,
    grad_key_out,
    grad_value_out,
    grad_decay_out,
    adjoint,
):
    count = key.shape[0] // BLOCK
    adjoint[...] = adjoint_in[...]
    later = lax.broadcasted_iota(jnp.int32, (BLOCK, BLOCK), 0)
    earlier = lax.broadcasted_iota(jnp.int32, (BLOCK, BLOCK), 1)
    upper = tri(BLOCK, False, 2)

    def step(turn, _):
        block = count - 1 - turn
        rows = pl.ds(pl.multiple_of(block * BLOCK, BLOCK), BLOCK)
        last, prev = block_ids(ids_s, prev_s, block)
        ids = ids_c[rows, :]
        linked = (ids == ids_r[pl.ds(block, 1), :]) & (later >= earlier)
        keep = (ids == last).astype(F32)
        alive = (ids == prev).astype(F32) * SCALE
        survive = (last == prev).astype(F32)
        total_all = total_in[rows, :]
        final_all = total_all[BLOCK - 1 : BLOCK, :]
        anchor_all = total_all[BLOCK // 2 : BLOCK // 2 + 1, :]
        for head in range(heads):
            kc = slice(head * KH, (head + 1) * KH)
            vc = slice(head * VH, (head + 1) * VH)
            total = total_all[:, kc]
            final = final_all[:, kc]
            anchor = anchor_all[:, kc]
            query_f = query[rows, kc].astype(F32)
            key_f = key[rows, kc].astype(F32)
            query_grow = SCALE * jnp.exp(total - anchor)
            key_grow = jnp.exp(anchor - total)
            reach_grow = jnp.exp(total) * alive
            tail_grow = jnp.exp(final - total) * keep
            through = survive * jnp.exp(final)
            query_scaled = (query_f * query_grow).astype(BF)
            key_scaled = (key_f * key_grow).astype(BF)
            reach = (query_f * reach_grow).astype(BF)
            tail = (key_f * tail_grow).astype(BF)
            value_rows = value[rows, vc]
            grad = grad_mixed[rows, vc]
            before = states[block, vc, :]
            after = adjoint[vc, :]
            after_b = after.astype(BF)
            scores = mm(query_scaled, key_scaled, 1, 1)
            scores = jnp.where(linked, scores, 0.0).astype(BF)
            grad_scores = mm(grad, value_rows, 1, 1)
            grad_scores = jnp.where(linked, grad_scores, 0.0).astype(BF)
            grad_query_scaled = mm(grad_scores, key_scaled)
            grad_key_scaled = mm(grad_scores, query_scaled, 0, 0)
            grad_reach = mm(grad, before)
            grad_tail = mm(value_rows, after_b)
            grad_query_out[rows, kc] = (
                grad_query_scaled * query_grow + grad_reach * reach_grow
            ).astype(BF)
            grad_key_out[rows, kc] = (grad_key_scaled * key_grow + grad_tail * tail_grow).astype(BF)
            grad_value_out[rows, vc] = (mm(scores, grad, 0, 0) + mm(tail, after_b, 1, 1)).astype(BF)
            tail_part = tail.astype(F32) * grad_tail
            grad_total = (
                query_scaled.astype(F32) * grad_query_scaled
                - key_scaled.astype(F32) * grad_key_scaled
                + reach.astype(F32) * grad_reach
                - tail_part
            )
            grad_final = jnp.sum(tail_part, axis=0, keepdims=True) + through * jnp.sum(
                before.astype(F32) * after, axis=0, keepdims=True
            )
            hi, low = split_hi_lo(grad_total)
            grad_decay_out[rows, kc] = (
                mm(upper, jnp.concatenate([hi, low], axis=0)) + grad_final
            )
            adjoint[vc, :] = after * through + mm(grad, reach, 0, 0)
        return 0

    lax.fori_loop(0, count, step, 0, unroll=2)


def call(kernel, outs, kinds, args, flops, scratch=()):
    spaces = {"s": pltpu.SMEM, "v": pltpu.VMEM}
    shapes = [jax.ShapeDtypeStruct(shape, kind) for shape, kind in outs]
    moved = sum(a.size * a.dtype.itemsize for a in list(args) + shapes)
    return pl.pallas_call(
        kernel,
        out_shape=shapes,
        in_specs=[pl.BlockSpec(memory_space=spaces[kind]) for kind in kinds],
        out_specs=[pl.BlockSpec(memory_space=pltpu.VMEM)] * len(outs),
        scratch_shapes=list(scratch),
        cost_estimate=pl.CostEstimate(flops=flops, bytes_accessed=moved, transcendentals=0),
        compiler_params=pltpu.CompilerParams(vmem_limit_bytes=VMEM_LIMIT),
    )(*args)


def ending_call(ids, prev, ids_col, key, value, decay):
    length, keys = key.shape
    heads = keys // KH
    return call(
        functools.partial(ending_kernel, heads),
        [((length, keys), F32), ((heads * VH, KH), F32), ((1, keys), F32)],
        "ssvvvv",
        (ids, prev, ids_col, key, value, decay),
        8 * 10**9,
    )


def forward_call(ids, prev, ids_col, ids_row, query, key, value, total, gate, gain, state):
    length, keys = key.shape
    heads = keys // KH
    return call(
        functools.partial(forward_kernel, heads),
        [
            ((length, heads * VH), F32),
            ((length, heads * VH), BF),
            ((length // BLOCK, heads * VH, KH), BF),
        ],
        "ssvvvvvvvvv",
        (ids, prev, ids_col, ids_row, query, key, value, total, gate, gain, state),
        20 * 10**9,
        [pltpu.VMEM((heads * VH, KH), F32)],
    )


def back_start_call(ids, prev, ids_col, query, total, gate, gain, mixed, grad_gated):
    length, keys = query.shape
    heads = keys // KH
    return call(
        functools.partial(back_start_kernel, heads),
        [
            ((length, heads * VH), BF),
            ((length, heads * VH), BF),
            ((1, VH), F32),
            ((heads * VH, KH), F32),
        ],
        "ssvvvvvvv",
        (ids, prev, ids_col, query, total, gate, gain, mixed, grad_gated),
        15 * 10**9,
    )


def backward_call(ids, prev, ids_col, ids_row, query, key, value, total, grad, states, adjoint):
    length, keys = key.shape
    heads = keys // KH
    return call(
        functools.partial(backward_kernel, heads),
        [
            ((length, keys), BF),
            ((length, keys), BF),
            ((length, heads * VH), BF),
            ((length, keys), F32),
        ],
        "ssvvvvvvvvv",
        (ids, prev, ids_col, ids_row, query, key, value, total, grad, states, adjoint),
        40 * 10**9,
        [pltpu.VMEM((heads * VH, KH), F32)],
    )


def swap(array, axis, bit):
    count = lax.axis_size(axis)
    return lax.ppermute(array, axis, [(i, i ^ bit) for i in range(count)])


def both(part):
    sent = part.astype(BF)
    return sent.astype(F32) + swap(sent, "tp", 1).astype(F32)


def pick(array, index, axis):
    return lax.dynamic_index_in_dim(array, index, axis, False)


def paired(mine, other, bit, axis):
    low = jnp.where(bit == 0, mine, other)
    high = jnp.where(bit == 0, other, mine)
    return jnp.stack([low, high], axis=axis)


def after(array, done):
    return array if done is None else lax.optimization_barrier((array, done))[0]


def along_ctx(array, late=None):
    place = lax.axis_index("ctx")
    x_bit, y_bit = place % 2, place // 2
    half = array.shape[0] // 2

    def x_first(part):
        row = paired(part, swap(part, "ctx", 1), x_bit, -3)
        whole = paired(row, after(swap(row, "ctx", 2), late), y_bit, -4)
        return whole.reshape(*part.shape[:-2], 4, *part.shape[-2:])

    def y_first(part):
        row = paired(part, swap(part, "ctx", 2), y_bit, -3)
        whole = paired(row, after(swap(row, "ctx", 1), late), x_bit, -3)
        return whole.reshape(*part.shape[:-2], 4, *part.shape[-2:])

    return jnp.concatenate([x_first(array[:half]), y_first(array[half:])], axis=0)


def gather_pieces(shard, done=None):
    rows, ctx = shard.shape[0], lax.axis_size("ctx")
    count = lax.axis_size("fsdp")
    part = lax.dynamic_slice_in_dim(shard, lax.axis_index("ctx") * (rows // ctx), rows // ctx, 0)
    part = after(part, done)
    if count > 4:
        return lax.all_gather(part, "fsdp", axis=0)
    place = lax.axis_index("fsdp")
    pieces = jnp.zeros((count, *part.shape), part.dtype)
    pieces = lax.dynamic_update_index_in_dim(pieces, part, place, 0)
    for shift in range(1, count):
        moved = lax.ppermute(part, "fsdp", [(i, (i + shift) % count) for i in range(count)])
        pieces = lax.dynamic_update_index_in_dim(pieces, moved, (place - shift) % count, 0)
    return pieces


def join_pieces(pieces, done=None, late=None):
    return along_ctx(after(pieces, done), late).reshape(-1, pieces.shape[-1])


def fold(array, bit, step, axis, late):
    theirs = after(swap(pick(array, 1 - bit, axis), "ctx", step), late)
    return (pick(array, bit, axis).astype(F32) + theirs.astype(F32)).astype(BF)


def ctx_bits():
    place = lax.axis_index("ctx")
    return place % 2, place // 2


def reduce_start(grad, late=None):
    rows, columns = grad.shape
    count, ctx = lax.axis_size("fsdp"), lax.axis_size("ctx")
    x_bit, y_bit = ctx_bits()
    blocks = grad.astype(BF).reshape(count, 2, 2, rows // (count * ctx), columns)
    half = count // 2
    return fold(blocks[:half], x_bit, 1, 2, late), fold(blocks[half:], y_bit, 2, 1, late)


def reduce_finish(started, late=None, late_last=None):
    count = lax.axis_size("fsdp")
    x_bit, y_bit = ctx_bits()
    first = fold(started[0], y_bit, 2, 1, late)
    second = fold(started[1], x_bit, 1, 1, late)
    partial = jnp.concatenate([first, second], axis=0)
    if count > 4:
        return lax.psum_scatter(partial, "fsdp", scatter_dimension=0, tiled=False)
    at = lax.axis_index("fsdp")
    total = pick(partial, at, 0).astype(F32)
    for shift in range(1, count):
        sent = pick(partial, (at + shift) % count, 0)
        moved = lax.ppermute(sent, "fsdp", [(i, (i + shift) % count) for i in range(count)])
        total = total + after(moved, late_last).astype(F32)
    return total.astype(BF)


def spread(own):
    size, columns = own.shape
    whole = along_ctx(own.reshape(2, size // 2, columns))
    return jnp.moveaxis(whole, 0, 1).reshape(-1, columns).astype(F32)


def shifted(value, axis, steps):
    count = lax.axis_size(axis)
    initial, last = (max(0, -steps), min(count, count - steps))
    return lax.ppermute(value, axis, [(source, source + steps) for source in range(initial, last)])


def dot(left, right, left_dim=1, right_dim=0):
    return lax.dot_general(
        left, right, (((left_dim,), (right_dim,)), ((), ())), preferred_element_type=F32
    )


def rms_scale(rows):
    return lax.rsqrt(jnp.mean(rows * rows, axis=-1, keepdims=True) + EPSILON)


def norm_back(grad_normed, rows, scale, gain):
    inner_term = gain * grad_normed
    return scale * (
        inner_term - rows * scale * scale * jnp.mean(inner_term * rows, axis=-1, keepdims=True)
    )


def carried(decay, state, step):
    heads = state.shape[0] // VH
    packed = jnp.concatenate([state, decay.reshape(heads, KH)], axis=0).astype(BF)
    out = jnp.zeros_like(state)
    moved = [shifted(packed, "ctx", step * far) for far in range(1, lax.axis_size("ctx"))]
    for piece in reversed(moved):
        piece = piece.astype(F32)
        grown = jnp.repeat(piece[heads * VH :], VH, axis=0)
        out = grown * out + piece[: heads * VH]
    return out


def sum_all(array):
    for axis in ("ctx", "fsdp"):
        count, bit = lax.axis_size(axis), 1
        if count & (count - 1):
            array = lax.psum(array, axis)
            continue
        while bit < count:
            array = array + swap(array, axis, bit)
            bit *= 2
    return array


def body(
    tokens,
    doc_ids,
    prenorm,
    w_query,
    w_key,
    w_value,
    w_outgate,
    w_lowrank,
    w_decay,
    decay_bias,
    headnorm,
    w_output,
    postnorm,
    w_gate,
    w_up,
    w_down,
    cotangent,
):
    keys, values = w_query.shape[1], w_value.shape[1]
    rank, hidden_size = w_lowrank.shape[1], w_gate.shape[1]
    heads = keys // KH
    mixer_size = 2 * keys + 2 * values
    extra = -(rank + 2) % 128
    pad = jnp.zeros((prenorm.shape[0], extra), BF)
    mixer_pack = jnp.concatenate(
        [w_query, w_key, w_value, w_outgate, w_lowrank, prenorm[:, None], postnorm[:, None], pad],
        axis=1,
    )
    mixer_pieces = gather_pieces(mixer_pack)
    ffn_pieces = gather_pieces(jnp.concatenate([w_gate, w_up, w_output.T], axis=1), mixer_pieces)
    down_pieces = gather_pieces(w_down.T, ffn_pieces)
    mixer_all = join_pieces(mixer_pieces)
    mat_lowrank = mixer_all[:, mixer_size : mixer_size + rank]
    gain_first = mixer_all[:, mixer_size + rank].astype(F32)
    gain_second = mixer_all[:, mixer_size + rank + 1].astype(F32)
    gain_head = headnorm.astype(F32)[None, :]

    ids = doc_ids[0]
    last_id = ids[-1:]
    prev_id = shifted(last_id, "ctx", 1)
    link = (last_id == prev_id).astype(F32)
    ids_col, ids_row = ids[:, None], ids.reshape(-1, BLOCK)

    resid_in = tokens[0].astype(F32)
    scale_one = rms_scale(resid_in)
    normed_one = (resid_in * scale_one * gain_first).astype(BF)
    projected = dot(normed_one, mixer_all)
    query = projected[:, :keys].astype(BF)
    key = projected[:, keys : 2 * keys].astype(BF)
    value = projected[:, 2 * keys : 2 * keys + values].astype(BF)
    gate_pre = projected[:, 2 * keys + values : mixer_size]
    rank_act = projected[:, mixer_size : mixer_size + rank].astype(BF)
    decay_logit = dot(rank_act, w_decay) + decay_bias.astype(F32)
    log_decay = jax.nn.log_sigmoid(decay_logit) / NORMALIZER

    total, ending, decay_sum = ending_call(ids, prev_id, ids_col, key, value, log_decay)
    through = jnp.exp(decay_sum) * link
    incoming = carried(through, ending, 1)
    mixed, gated, states = forward_call(
        ids, prev_id, ids_col, ids_row, query, key, value, total, gate_pre, gain_head, incoming
    )

    ffn_all = join_pieces(ffn_pieces, projected, gated)
    mat_ffn, mat_output_t = ffn_all[:, : 2 * hidden_size], ffn_all[:, 2 * hidden_size :]
    resid_mid = resid_in + both(dot(gated, mat_output_t, 1, 1))
    scale_two = rms_scale(resid_mid)
    normed_two = (resid_mid * scale_two * gain_second).astype(BF)
    acts = dot(normed_two, mat_ffn)
    mat_down_t = join_pieces(down_pieces, ffn_all, acts)
    gate_act, up_act = acts[:, :hidden_size], acts[:, hidden_size:]
    ffn_sig = jax.nn.sigmoid(gate_act)
    silu_act = gate_act * ffn_sig
    hidden = (silu_act * up_act).astype(BF)
    block_out = (resid_mid + both(dot(hidden, mat_down_t, 1, 1))).astype(BF)
    cot = cotangent[0]
    grad_down = dot(cot, hidden, 0, 0).astype(BF)
    grad_hidden = dot(after(cot, grad_down), mat_down_t)
    grad_gate_act = (grad_hidden * up_act * ffn_sig * (1.0 + gate_act * (1.0 - ffn_sig))).astype(BF)
    grad_up_act = (grad_hidden * silu_act).astype(BF)
    grad_acts = jnp.concatenate([grad_gate_act, grad_up_act], axis=1)
    norm_two_grad = both(dot(grad_acts, mat_ffn, 1, 1))
    down_started = reduce_start(grad_down)
    grad_ffn = dot(after(normed_two, down_started), grad_acts, 0, 0).astype(BF)
    grad_ffn = after(grad_ffn, norm_two_grad)
    grad_postnorm = jnp.sum(norm_two_grad * resid_mid * scale_two, axis=0)
    grad_mid = cot.astype(F32) + norm_back(norm_two_grad, resid_mid, scale_two, gain_second)
    grad_attn = grad_mid.astype(BF)
    grad_gated = dot(grad_attn, mat_output_t)

    grad_mixed, grad_gate_rows, headnorm_part, adjoint = back_start_call(
        ids, prev_id, ids_col, query, total, gate_pre, gain_head, mixed, grad_gated
    )
    adjoint_in = carried(through, adjoint, -1)
    grad_query, grad_key, grad_value, grad_log_decay = backward_call(
        ids, prev_id, ids_col, ids_row, query, key, value, total, grad_mixed, states, adjoint_in
    )
    grad_logit = (grad_log_decay * jax.nn.sigmoid(-decay_logit) / NORMALIZER).astype(BF)
    grad_decay = dot(rank_act, grad_logit, 0, 0)
    grad_bias = jnp.sum(grad_logit.astype(F32), axis=0, keepdims=True)
    grad_rank = both(dot(grad_logit, w_decay, 1, 1)).astype(BF)
    grad_heads = jnp.concatenate([grad_query, grad_key, grad_value, grad_gate_rows], axis=1)
    grad_mixer = jnp.concatenate(
        [dot(normed_one, grad_heads, 0, 0).astype(BF), dot(grad_attn, gated, 0, 0).astype(BF)],
        axis=1,
    )
    grad_lowrank = dot(grad_rank, normed_one, 0, 0)
    norm_one_grad = both(dot(grad_heads, mixer_all[:, :mixer_size], 1, 1))
    norm_one_grad = norm_one_grad + dot(grad_rank, mat_lowrank, 1, 1)
    grad_prenorm = jnp.sum(norm_one_grad * resid_in * scale_one, axis=0)
    grad_tokens = (grad_mid + norm_back(norm_one_grad, resid_in, scale_one, gain_first)).astype(BF)
    down_own = reduce_finish(down_started, grad_attn, grad_query)
    ffn_own = reduce_finish(reduce_start(grad_ffn, grad_mixed), grad_query)
    wide_own = spread(jnp.concatenate([ffn_own, down_own], axis=1))
    heads_own = spread(reduce_finish(reduce_start(grad_mixer)))
    width = tokens.shape[2]
    tall = jnp.concatenate([grad_lowrank, grad_prenorm[None], grad_postnorm[None]], axis=0)
    narrow = jnp.concatenate([grad_decay, grad_bias, both(headnorm_part)], axis=0)
    sums = sum_all(jnp.concatenate([tall, narrow], axis=1))
    rows = prenorm.shape[0]
    small_own = lax.dynamic_slice_in_dim(sums, lax.axis_index("fsdp") * rows, rows, 1)
    narrow = sums[:, width:]
    return (
        block_out[None],
        grad_tokens[None],
        small_own[rank],
        heads_own[:, :keys],
        heads_own[:, keys : 2 * keys],
        heads_own[:, 2 * keys : 2 * keys + values],
        heads_own[:, 2 * keys + values : mixer_size],
        small_own[:rank].T,
        narrow[:rank],
        narrow[rank],
        narrow[rank + 1],
        heads_own[:, mixer_size:].T,
        small_own[rank + 1],
        wide_own[:, :hidden_size],
        wide_own[:, hidden_size : 2 * hidden_size],
        wide_own[:, 2 * hidden_size :].T,
    )


def solution(mesh):
    in_specs = (
        P("fsdp", "ctx", None),
        P("fsdp", "ctx"),
        P("fsdp"),
        P("fsdp", "tp"),
        P("fsdp", "tp"),
        P("fsdp", "tp"),
        P("fsdp", "tp"),
        P("fsdp", None),
        P(None, "tp"),
        P("tp"),
        P(),
        P("tp", "fsdp"),
        P("fsdp"),
        P("fsdp", "tp"),
        P("fsdp", "tp"),
        P("tp", "fsdp"),
        P("fsdp", "ctx", None),
    )
    out_specs = (
        P("fsdp", "ctx", None),
        P("fsdp", "ctx", None),
        P("fsdp"),
        P("fsdp", "tp"),
        P("fsdp", "tp"),
        P("fsdp", "tp"),
        P("fsdp", "tp"),
        P("fsdp", None),
        P(None, "tp"),
        P("tp"),
        P(),
        P("tp", "fsdp"),
        P("fsdp"),
        P("fsdp", "tp"),
        P("fsdp", "tp"),
        P("tp", "fsdp"),
    )
    return jax.shard_map(body, mesh=mesh, in_specs=in_specs, out_specs=out_specs, check_vma=False)
```
